256 devices in a mesh: grp: 8 (over x, z_hi), mem: 32 (over y, z_lo, core).
Axes of the slice: x: 4, y: 4, z: 8 (z_hi: 2, z_lo: 4; z = z_hi * 4 + z_lo), core: 2. Of those that a mesh axis runs over, the one named last changes fastest.
Arguments:
- initial_state: bfloat16 [128, 128, 64, 2, 128], P('grp', 'mem'), may hold values from -6 to 6
- cotangent: bfloat16 [128, 128, 64, 2, 128], P('grp', 'mem'), may hold values from -6 to 6
- gate_bank: bfloat16 [3, 4, 2, 128, 128], replicated, may hold values from -0.375 to 0.375
- slice_index: int32 [3], replicated, may hold values from 0 to 3
- mode_order: int32 [3, 7], replicated, may hold values from 0 to 6, each once within a row
Outputs:
- gate_grads: float32 [3, 2, 128, 128], replicated
- state_grad: bfloat16 [128, 128, 64, 2, 128], P('grp', None, 'mem')
The draws below stay inside these ranges and needn't reach their ends.
Inputs may be any that keep to these rules, and one draw needn't show every extreme that they name: `mode_order`: each row names every position 0 to 6 once.
All inputs are finite; a program needn't handle non-finite values.
Results may differ from the reference program's by a relative error of at most 0.0057.
Values may be sent and summed in bfloat16 or wider, within the bound.
A program may use at most 64 MiB of HBM per device.

```python
from functools import partial
import jax
import jax.numpy as jnp
from jax import lax

QB = 7
KW = 128
RL = 64
SLICES = 4


def block_scale(key, shape, cuts, least, largest):
    gain, own = 1.0, jax.random.fold_in(key, 6)
    for dim, shards_of in cuts:
        heights = jnp.exp(jax.random.uniform(jax.random.fold_in(own, dim), (shards_of,), jnp.float32, least / len(cuts), largest / len(cuts)))
        gain = gain * jnp.repeat(heights, shape[dim] // shards_of).reshape([-1 if axis == dim else 1 for axis in range(len(shape))])
    return gain


def noise(key, shape, spread, reach, cuts=(), kind=jnp.bfloat16):
    values = jax.random.normal(key, shape, jnp.float32) * spread
    if len(cuts) > 0:
        values = block_scale(key, shape, cuts, -0.22, 0.18) * values
    return jnp.clip(values, min=-reach, max=reach).astype(kind)


def setup_inputs(seed: int = 0) -> dict:
    key_list = jax.random.split(jax.random.key(seed), 6)
    return {
        "initial_state": noise(key_list[0], (KW, KW, RL, 2, KW), 1.0, 6.0, ((0, 8), (1, 32))),
        "cotangent": noise(key_list[1], (KW, KW, RL, 2, KW), 1.0, 6.0, ((0, 8), (1, 32))),
        "gate_bank": noise(key_list[2], (3, SLICES, 2, KW, KW), (2 * KW) ** -0.5, 0.375),
        "slice_index": jax.random.randint(key_list[3], (3,), 0, SLICES).astype(jnp.int32),
        "mode_order": jax.vmap(lambda own: jax.random.permutation(own, QB))(jax.random.split(key_list[4], 3)).reshape((3, QB)).astype(jnp.int32),
    }


block_rows = 8


def index_table(order_row):
    states = jnp.arange(KW, dtype=jnp.int32)
    places = jnp.arange(QB, dtype=jnp.int32)
    bits = (states[:, None] >> places[None, :]) & 1
    mapped = jnp.sum(bits << order_row[None, :], axis=1).astype(jnp.int32)
    return (mapped[:, None] == states[None, :]).astype(jnp.float32)


def gate_matrix(gate_bank, slice_index, mode_order, number):
    chosen = lax.dynamic_index_in_dim(gate_bank[number], slice_index[number], 0, keepdims=False).astype(jnp.float32)
    picker = index_table(mode_order[number])
    moved = jnp.matmul(jnp.matmul(picker, chosen, precision=lax.Precision.HIGHEST), picker.T, precision=lax.Precision.HIGHEST)
    upper = jnp.stack([moved[0], -moved[1]], axis=1)
    lower = jnp.stack([moved[1], moved[0]], axis=1)
    return jnp.stack([upper, lower], axis=0).astype(jnp.bfloat16), picker


def fold_planes(grad_real):
    return jnp.stack([grad_real[0, :, 0, :] + grad_real[1, :, 1, :], grad_real[1, :, 0, :] - grad_real[0, :, 1, :]])


def reference(initial_state, cotangent, gate_bank, slice_index, mode_order):
    mats = [gate_matrix(gate_bank, slice_index, mode_order, number) for number in range(3)]
    first = mats[0][0].astype(jnp.float32)
    second = mats[1][0].astype(jnp.float32)
    third = mats[2][0].astype(jnp.float32)
    contract = partial(jnp.einsum, precision=lax.Precision.HIGHEST)

    def block(carry, number):
        start = (number * block_rows).astype(jnp.int32)
        initial = lax.dynamic_slice_in_dim(initial_state, start, block_rows, 2).astype(jnp.float32)
        outer = lax.dynamic_slice_in_dim(cotangent, start, block_rows, 2).astype(jnp.float32)
        layer_one = contract('nmrdj,cidj->nmrci', initial, first).astype(jnp.bfloat16).astype(jnp.float32)
        layer_two = contract('njrdk,cidj->nirck', layer_one, second).astype(jnp.bfloat16).astype(jnp.float32)
        back_two = contract('imrck,cidj->jmrdk', outer, third).astype(jnp.bfloat16).astype(jnp.float32)
        back_one = contract('nirck,cidj->njrdk', back_two, second).astype(jnp.bfloat16).astype(jnp.float32)
        grad_block = contract('nmrci,cidj->nmrdj', back_one, first).astype(jnp.bfloat16)
        grad_three = fold_planes(contract('imrck,jmrdk->cidj', outer, layer_two))
        grad_two = fold_planes(contract('nirck,njrdk->cidj', back_two, layer_one))
        grad_one = fold_planes(contract('nmrci,nmrdj->cidj', back_one, initial))
        carry = (carry[0] + grad_one, carry[1] + grad_two, carry[2] + grad_three)
        return carry, grad_block

    zeros = jnp.zeros((2, KW, KW), jnp.float32)
    totals, blocks = lax.scan(block, (zeros, zeros, zeros), jnp.arange(RL // block_rows, dtype=jnp.int32))
    state_grad = jnp.moveaxis(blocks, 0, 2).reshape(KW, KW, RL, 2, KW)
    factor = 1.0 / (KW * (RL ** 0.5))
    grads = []
    for number in range(3):
        picker = mats[number][1]
        restored = jnp.matmul(jnp.matmul(picker.T, totals[number], precision=lax.Precision.HIGHEST), picker, precision=lax.Precision.HIGHEST)
        grads.append(restored * factor)
    return jnp.stack(grads), state_grad
```

```python
import numpy as np
import jax
import jax.numpy as jnp
from jax import lax
from jax.experimental import pallas as pl
from jax.experimental.pallas import tpu as pltpu
from jax.sharding import PartitionSpec as P

MESH = pl.DeviceIdType.MESH
BF = jnp.bfloat16
F32 = jnp.float32
HIGH = lax.Precision.HIGHEST
NX, NY, NZ, NC = 4, 4, 8, 2
Z_ORDER = (4, 3, 5, 2, 6, 1, 7, 0)


def block_turn():
    mat = np.zeros((256, 256), np.float32)
    for a in range(16):
        for b in range(16):
            mat[b * 16 + a, a * 16 + b] = 1.0
    return mat


def stored_order():
    order = np.zeros(128, np.int32)
    for y in range(4):
        for c in range(2):
            for zl in range(4):
                for ml in range(4):
                    order[y * 32 + c * 16 + zl * 4 + ml] = ((y * 4 + zl) * 2 + c) * 4 + ml
    return order


def output_turn():
    order = stored_order()
    mat = np.zeros((256, 256), np.float32)
    for s in range(64):
        for rc in range(4):
            mat[order[s] * 4 + rc, rc * 64 + s] = 1.0
    return mat


def index_table(order_row, width):
    places_count = order_row.shape[0]
    states = jnp.arange(width, dtype=jnp.int32)
    places = jnp.arange(places_count, dtype=jnp.int32)
    bits = states[:, None] >> places[None, :] & 1
    mapped = jnp.sum(bits << order_row[None, :], axis=1)
    return (mapped[:, None] == states[None, :]).astype(F32)


def gate_matrix(gate_bank, slice_index, mode_order, number):
    width = gate_bank.shape[-1]
    chosen = lax.dynamic_index_in_dim(gate_bank[number], slice_index[number], 0, keepdims=False)
    picker = index_table(mode_order[number], width)
    small = picker.astype(BF)
    moved = jnp.einsum("ia,qab,jb->qij", small, chosen, small, preferred_element_type=F32).astype(BF)
    upper = jnp.stack([moved[0], -moved[1]], axis=1)
    lower = jnp.stack([moved[1], moved[0]], axis=1)
    return jnp.stack([upper, lower], axis=0), picker


def dot(a, b):
    return jnp.dot(a, b, preferred_element_type=F32)


def dot_nt(a, b):
    return lax.dot_general(a, b, (((1,), (1,)), ((), ())), preferred_element_type=F32)


def dot_tn(a, b):
    return lax.dot_general(a, b, (((0,), (0,)), ((), ())), preferred_element_type=F32)


def planes_down(a, b):
    top = jnp.concatenate([a[:, :128], b[:, :128]], axis=1)
    low = jnp.concatenate([a[:, 128:], b[:, 128:]], axis=1)
    return jnp.concatenate([top, low], axis=0)


def planes_up(o, which):
    half = o.shape[0] // 2
    lanes = slice(128 * which, 128 * which + 128)
    return jnp.concatenate([o[:half, lanes], o[half:, lanes]], axis=1)


def with_turned(l):
    return jnp.concatenate([l, jnp.concatenate([-l[:, 128:], l[:, :128]], axis=1)], axis=0)


def kernel(
    craw, xraw, w1f, w1b, w2f, w2b, w3b, turn, outturn, pickers,
    out, eout,
    csend, xsend, call, xq, b2, b2t, b1t, sg, xt, l1t, l2t, sgr, v1acc, e, rx, ryc, rz, fin,
    c_ss, c_rs, x_ss, x_rs, loc, g_ss, g_rs, f_ss, f_rs, s_ss, s_rs,
    e1s, e1r, e2s, e2r, e3s, e3r, e4s, e4r, e5s, e5r,
):
    grp, mem = lax.axis_index("grp"), lax.axis_index("mem")
    x, zh = grp // 2, grp % 2
    y, zl, c = mem // 8, (mem // 2) % 4, mem % 2
    z = zh * 4 + zl

    def device(dx, dy, dz, dc):
        x2, y2, z2, c2 = (x + dx) % NX, (y + dy) % NY, (z + dz) % NZ, (c + dc) % NC
        return (x2 * 2 + z2 // 4, (y2 * 4 + z2 % 4) * 2 + c2)

    def yzc(t):
        return t // 16, t % 8, (t // 8) % 2

    bar = pltpu.get_barrier_semaphore()

    def greet(t, carry):
        dy, dz, dc = yzc(t)
        pl.semaphore_signal(bar, inc=1, device_id=device(0, dy, dz, dc), device_id_type=MESH)
        return carry

    lax.fori_loop(1, 64, greet, 0)
    for dx in range(1, NX):
        pl.semaphore_signal(bar, inc=1, device_id=device(dx, 0, 0, 0), device_id_type=MESH)

    def extract(raw, send):
        def body(i, carry):
            mp, rb = i // 8, i % 8
            rows = pl.ds(pl.multiple_of(16 * rb, 16), 16)
            a = raw[:, 2 * mp, rows, :].reshape(256, 128)
            b = raw[:, 2 * mp + 1, rows, :].reshape(256, 128)
            o = dot(turn[...], jnp.concatenate([a, b], axis=1)).astype(BF)
            for mm in range(2):
                for r in range(8):
                    for cc in range(2):
                        q = (r * 2 + cc) * 16
                        send[8 * rb + r, 2 * mp + mm, :, cc * 128:cc * 128 + 128] = o[q:q + 16, mm * 128:mm * 128 + 128]
            return carry

        lax.fori_loop(0, 16, body, 0)

    extract(craw, csend)
    pl.semaphore_wait(bar, 66)

    m_own = pl.multiple_of(y * 32 + c * 16 + zl * 4, 4)
    n_own = pl.multiple_of(32 * x + 16 * zh, 16)
    nq_own = pl.multiple_of(16 * zh, 16)

    def part_of(dy, dz, dc):
        s = (z + dz + 6) % NZ
        return 2 * ((((y + dy) % NY) * 4 + s % 4) * 2 + (c + dc) % NC) + s // 4

    def c_copy(t):
        dy, dz, dc = yzc(t)
        return pltpu.make_async_remote_copy(
            src_ref=csend.at[part_of(dy, dz, dc)],
            dst_ref=call.at[pl.ds(m_own, 4), pl.ds(n_own, 16), :],
            send_sem=c_ss.at[t], recv_sem=c_rs.at[t],
            device_id=device(0, dy, dz, dc), device_id_type=MESH)

    def x_copy(t):
        dy, dz, dc = yzc(t)
        return pltpu.make_async_remote_copy(
            src_ref=xsend.at[part_of(dy, dz, dc)],
            dst_ref=xq.at[pl.ds(m_own, 4), pl.ds(nq_own, 16), :],
            send_sem=x_ss.at[t], recv_sem=x_rs.at[t],
            device_id=device(0, dy, dz, dc), device_id_type=MESH)

    own_c = pltpu.make_async_copy(csend.at[part_of(0, 0, 0)], call.at[pl.ds(m_own, 4), pl.ds(n_own, 16), :], loc.at[0])
    own_x = pltpu.make_async_copy(xsend.at[part_of(0, 0, 0)], xq.at[pl.ds(m_own, 4), pl.ds(nq_own, 16), :], loc.at[1])

    def start_group(copy, g):
        for dz in Z_ORDER:
            if dz == 0:
                @pl.when(g > 0)
                def _():
                    copy(g * 8).start()
            else:
                copy(g * 8 + dz).start()

    def c_start(g, carry):
        start_group(c_copy, g)
        return carry

    own_c.start()
    lax.fori_loop(0, 8, c_start, 0)
    extract(xraw, xsend)
    own_x.start()

    def m_of(g):
        dy, dc = g // 2, g % 2
        return pl.multiple_of(((y + NY - dy) % NY) * 32 + ((c + NC - dc) % NC) * 16, 16)

    def near(g, way):
        part = call.at[pl.ds(m_of(g), 16), pl.ds(pl.multiple_of(32 * x, 32), 32), :]
        return pltpu.make_async_remote_copy(
            src_ref=part, dst_ref=part, send_sem=g_ss.at[way, g], recv_sem=g_rs.at[way, g],
            device_id=device(1 if way == 0 else NX - 1, 0, 0, 0), device_id_type=MESH)

    def far(g, way):
        owner = (x + NX - 1) % NX if way == 0 else (x + 1) % NX
        part = call.at[pl.ds(m_of(g) + 8 * way, 8), pl.ds(pl.multiple_of(32 * owner, 32), 32), :]
        return pltpu.make_async_remote_copy(
            src_ref=part, dst_ref=part, send_sem=f_ss.at[way, g], recv_sem=f_rs.at[way, g],
            device_id=device(1 if way == 0 else NX - 1, 0, 0, 0), device_id_type=MESH)

    def relay(g):
        for way in range(2):
            near(g, way).wait_recv()
            far(g, way).start()

    def arrive(g, carry):
        for dz in Z_ORDER:
            if dz == 0:
                @pl.when(g > 0)
                def _():
                    c_copy(g * 8).wait_recv()
            else:
                c_copy(g * 8 + dz).wait_recv()

        @pl.when(g == 0)
        def _():
            own_c.wait()

        near(g, 0).start()
        near(g, 1).start()

        @pl.when(g >= 4)
        def _():
            start_group(x_copy, (g - 4) * 2)
            start_group(x_copy, (g - 4) * 2 + 1)

        @pl.when(g >= 1)
        def _():
            relay(g - 1)

        return carry

    lax.fori_loop(0, 8, arrive, 0)
    relay(7)

    def third(g, carry):
        far(g, 0).wait_recv()
        far(g, 1).wait_recv()
        base = m_of(g)
        for p in range(8):
            m = base + 2 * p
            o = dot(w3b[...], planes_down(call[m], call[m + 1])).astype(BF)
            b2[m] = planes_up(o, 0)
            b2[m + 1] = planes_up(o, 1)
        return carry

    lax.fori_loop(0, 8, third, 0)

    def turn_block(src, dst, half, i, to_rows):
        at = pl.ds(pl.multiple_of(16 * i, 16), 16)
        cols = slice(16 * half, 16 * half + 16)
        if to_rows:
            blk = src[at, cols, :]
        else:
            blk = src[cols, at, :]
        o = dot(turn[...], blk.reshape(256, 256)).astype(BF).reshape(16, 16, 256)
        if to_rows:
            dst[cols, at, :] = o
        else:
            dst[at, cols, :] = o

    def gate_two(src, dst, w, n):
        o = dot(w[...], planes_down(src[n], src[n + 1])).astype(BF)
        dst[n] = planes_up(o, 0)
        dst[n + 1] = planes_up(o, 1)

    def gate_one(src, dst, w, n):
        o = dot(src[pl.ds(n, 2)].reshape(256, 256), w[...]).astype(BF)
        dst[pl.ds(n, 2)] = o.reshape(2, 128, 256)

    s_here = (z + 6) % NZ
    part_here = s_here // 4

    def back(half):
        z_to = 4 * half + s_here % 4
        return pltpu.make_async_remote_copy(
            src_ref=sg.at[pl.ds(16 * half, 16)], dst_ref=sgr.at[part_here],
            send_sem=s_ss.at[half], recv_sem=s_rs.at[part_here],
            device_id=device(0, 0, z_to + NZ - z, 0), device_id_type=MESH)

    for half in range(2):
        def turned(i, carry, half=half):
            turn_block(b2, b2t, half, i, True)
            return carry

        def gates(i, carry, half=half):
            n = 16 * half + 2 * i
            gate_two(b2t, b1t, w2b, n)
            gate_one(b1t, sg, w1b, n)
            return carry

        lax.fori_loop(0, 8, turned, 0)
        lax.fori_loop(0, 8, gates, 0)
        back(half).start()

    def x_arrive(t, carry):
        x_copy(t).wait_recv()
        return carry

    own_x.wait()
    lax.fori_loop(1, 64, x_arrive, 0)

    for half in range(2):
        def x_turned(i, carry, half=half):
            turn_block(xq, xt, half, i, True)
            return carry

        lax.fori_loop(0, 8, x_turned, 0)

    def layers(i, carry):
        gate_one(xt, l1t, w1f, 2 * i)
        gate_two(l1t, l2t, w2f, 2 * i)
        return carry

    lax.fori_loop(0, 16, layers, 0)

    for half in range(2):
        def l_turned(i, carry, half=half):
            turn_block(l2t, b2, half, i, False)
            return carry

        lax.fori_loop(0, 8, l_turned, 0)

    def grad_two(n, acc):
        return acc + dot_nt(b2t[n], with_turned(l1t[n]))

    acc = lax.fori_loop(0, 32, grad_two, jnp.zeros((128, 256), F32))
    e[256:384, :] = acc[:, :128]
    e[384:512, :] = acc[:, 128:]

    v1acc[...] = jnp.zeros_like(v1acc)

    def grad_one(i, carry):
        rows = pl.ds(4 * i, 4)
        v1acc[...] += dot_tn(b1t[rows].reshape(512, 256), xt[rows].reshape(512, 256))
        return carry

    lax.fori_loop(0, 8, grad_one, 0)
    e[0:128, :] = v1acc[0:128, 0:128] + v1acc[128:256, 128:256]
    e[128:256, :] = v1acc[128:256, 0:128] - v1acc[0:128, 128:256]

    def grad_three(i, acc):
        for p in range(4):
            m = 4 * i + p
            acc = acc + dot_nt(call[m], with_turned(b2[m]))
        return acc

    acc3 = lax.fori_loop(0, 32, grad_three, jnp.zeros((128, 64), F32))
    acc3 = jnp.transpose(jnp.concatenate([acc3, jnp.zeros((128, 64), F32)], axis=1))
    e[512:768, :] = jnp.zeros((256, 128), F32)
    spot = pl.multiple_of(32 * x, 32)
    e[pl.ds(512 + spot, 32), :] = acc3[0:32, :]
    e[pl.ds(640 + spot, 32), :] = acc3[32:64, :]

    def one(dx):
        to = (x + dx) % NX
        return pltpu.make_async_remote_copy(
            src_ref=e.at[pl.ds(pl.multiple_of(192 * to, 192), 192), :], dst_ref=rx.at[x],
            send_sem=e1s.at[dx], recv_sem=e1r.at[dx], device_id=device(dx, 0, 0, 0), device_id_type=MESH)

    def yc(k):
        return ((y + k // 2) % NY) * 2 + (c + k % 2) % NC

    def two(k):
        to = yc(k)
        return pltpu.make_async_remote_copy(
            src_ref=ryc.at[8, pl.ds(pl.multiple_of(24 * to, 8), 24), :],
            dst_ref=ryc.at[y * 2 + c, pl.ds(0, 24), :],
            send_sem=e2s.at[k], recv_sem=e2r.at[k], device_id=device(0, k // 2, 0, k % 2), device_id_type=MESH)

    def three(dz):
        return pltpu.make_async_remote_copy(
            src_ref=rz.at[z], dst_ref=rz.at[z],
            send_sem=e3s.at[dz], recv_sem=e3r.at[dz], device_id=device(0, 0, dz, 0), device_id_type=MESH)

    def four(k):
        rows = fin.at[pl.ds(pl.multiple_of(192 * x + 24 * (y * 2 + c), 8), 24), :]
        return pltpu.make_async_remote_copy(
            src_ref=rows, dst_ref=rows,
            send_sem=e4s.at[k], recv_sem=e4r.at[k], device_id=device(0, k // 2, 0, k % 2), device_id_type=MESH)

    def five(dx):
        rows = fin.at[pl.ds(pl.multiple_of(192 * x, 192), 192), :]
        return pltpu.make_async_remote_copy(
            src_ref=rows, dst_ref=rows,
            send_sem=e5s.at[dx], recv_sem=e5r.at[dx], device_id=device(dx, 0, 0, 0), device_id_type=MESH)

    for dx in range(1, NX):
        one(dx).start()
    rx[x] = e[pl.ds(pl.multiple_of(192 * x, 192), 192), :]
    for dx in range(1, NX):
        one(dx).wait_recv()
    ryc[8] = (rx[0] + rx[1]) + (rx[2] + rx[3])
    for k in range(1, 8):
        two(k).start()
    ryc[y * 2 + c, 0:24, :] = ryc[8, pl.ds(pl.multiple_of(24 * (y * 2 + c), 8), 24), :]
    for k in range(1, 8):
        two(k).wait_recv()
    total = ryc[0, 0:24, :]
    for k in range(1, 8):
        total = total + ryc[k, 0:24, :]
    rz[z] = total
    for dz in range(1, NZ):
        three(dz).start()
    for dz in range(1, NZ):
        three(dz).wait_recv()
    total = rz[0]
    for k in range(1, NZ):
        total = total + rz[k]
    fin[pl.ds(pl.multiple_of(192 * x + 24 * (y * 2 + c), 8), 24), :] = total
    for k in range(1, 8):
        four(k).start()
    for k in range(1, 8):
        four(k).wait_recv()
    for dx in range(1, NX):
        five(dx).start()
    for dx in range(1, NX):
        five(dx).wait_recv()

    def exact(a, b, dims):
        return lax.dot_general(a, b, (dims, ((), ())), precision=HIGH, preferred_element_type=F32)

    factor = 1.0 / (128 * 64**0.5)
    for q in range(2):
        for s in range(2):
            part = fin[256 * s + 128 * q:256 * s + 128 * q + 128, :]
            moved = exact(pickers[s], part, ((0,), (0,)))
            eout[s, q] = exact(moved, pickers[s], ((1,), (0,))) * factor
        part = fin[512 + 128 * q:640 + 128 * q, :]
        moved = exact(pickers[2], part, ((0,), (1,)))
        eout[2, q] = exact(moved, pickers[2], ((1,), (0,))) * factor

    def c_gone(t, carry):
        c_copy(t).wait_send()
        x_copy(t).wait_send()
        return carry

    lax.fori_loop(1, 64, c_gone, 0)

    def g_gone(g, carry):
        for way in range(2):
            near(g, way).wait_send()
            far(g, way).wait_send()
        return carry

    lax.fori_loop(0, 8, g_gone, 0)
    for dx in range(1, NX):
        one(dx).wait_send()
        five(dx).wait_send()
    for k in range(1, 8):
        two(k).wait_send()
        three(k).wait_send()
        four(k).wait_send()

    def landed(part):
        return pltpu.make_async_remote_copy(
            src_ref=sg.at[pl.ds(0, 16)], dst_ref=sgr.at[part],
            send_sem=s_ss.at[0], recv_sem=s_rs.at[part],
            device_id=device(0, 0, 2, 0), device_id_type=MESH)

    landed(0).wait_recv()
    landed(1).wait_recv()

    def give(i, carry):
        n, hh = 2 * (i // 2), i % 2
        rows = pl.ds(pl.multiple_of(64 * hh, 64), 64)
        sides = []
        for nn in range(2):
            sides.append(jnp.concatenate(
                [sgr[r, n + nn, rows, cc * 128:cc * 128 + 128] for r in range(2) for cc in range(2)], axis=0))
        o = dot(outturn[...], jnp.concatenate(sides, axis=1)).astype(BF)
        at = pl.ds(pl.multiple_of(256 * hh, 256), 256)
        out[n, at, :] = o[:, :128]
        out[n + 1, at, :] = o[:, 128:]
        return carry

    lax.fori_loop(0, 16, give, 0)
    back(0).wait_send()
    back(1).wait_send()


def local(initial_state, cotangent, gate_bank, slice_index, mode_order):
    mats = [gate_matrix(gate_bank, slice_index, mode_order, number) for number in range(3)]
    first, second, third = mats[0][0], mats[1][0], mats[2][0]
    order = stored_order()
    second = second.reshape(2, 4, 4, 2, 4, 2, 4, 4, 2, 4).transpose(0, 1, 3, 2, 4, 5, 6, 8, 7, 9).reshape(256, 256)
    x = lax.axis_index("grp") // 2
    own = lax.dynamic_slice_in_dim(third, 32 * x, 32, 3)
    w3b = own.transpose(2, 3, 0, 1).reshape(64, 256)
    first = first.reshape(256, 256)
    pick_two = mats[1][1].reshape(4, 4, 2, 4, 128).transpose(0, 2, 1, 3, 4).reshape(128, 128)
    pickers = jnp.stack([mats[0][1], pick_two, mats[2][1]])
    del order
    vm = pl.BlockSpec(memory_space=pltpu.VMEM)
    big = lambda *shape: pltpu.VMEM(shape, BF)
    sem = lambda *shape: pltpu.SemaphoreType.DMA(shape)
    out, grads = pl.pallas_call(
        kernel,
        out_shape=(jax.ShapeDtypeStruct((16, 512, 128), BF), jax.ShapeDtypeStruct((3, 2, 128, 128), F32)),
        in_specs=[vm] * 10,
        out_specs=(vm, vm),
        scratch_shapes=[
            big(64, 4, 16, 256), big(64, 4, 16, 256), big(128, 128, 256), big(128, 32, 256),
            big(128, 32, 256), big(32, 128, 256), big(32, 128, 256), big(32, 128, 256),
            big(32, 128, 256), big(32, 128, 256), big(32, 128, 256), big(2, 16, 128, 256),
            pltpu.VMEM((256, 256), F32), pltpu.VMEM((768, 128), F32), pltpu.VMEM((4, 192, 128), F32),
            pltpu.VMEM((9, 192, 128), F32), pltpu.VMEM((8, 24, 128), F32), pltpu.VMEM((768, 128), F32),
            sem(64), sem(64), sem(64), sem(64), sem(2), sem(2, 8), sem(2, 8), sem(2, 8), sem(2, 8), sem(2), sem(2),
            sem(4), sem(4), sem(8), sem(8), sem(8), sem(8), sem(8), sem(8), sem(4), sem(4),
        ],
        compiler_params=pltpu.CompilerParams(collective_id=0, has_side_effects=True, vmem_limit_bytes=56 << 20),
        name="gradients",
    )(
        cotangent.reshape(16, 4, 128, 128), initial_state.reshape(16, 4, 128, 128),
        first.T, first, second, second.T, w3b,
        jnp.asarray(block_turn(), BF), jnp.asarray(output_turn(), BF), pickers,
    )
    return grads, out.reshape(16, 128, 2, 2, 128)


def solution(mesh):
    in_specs = (P("grp", "mem", None, None, None), P("grp", "mem", None, None, None), P(), P(), P())
    out_specs = (P(), P("grp", None, "mem", None, None))
    return jax.shard_map(local, mesh=mesh, in_specs=in_specs, out_specs=out_specs, check_vma=False)
```

```python
import jax
import jax.numpy as jnp
from jax import lax
from jax.experimental import pallas as pl
from jax.experimental.pallas import tpu as pltpu
from jax.sharding import PartitionSpec as P

MESH = pl.DeviceIdType.MESH
BF = jnp.bfloat16
F32 = jnp.float32
HIGH = lax.Precision.HIGHEST
NX, NY, NZ, NC = 4, 4, 8, 2
Z_ORDER = (4, 3, 5, 2, 6, 1, 7, 0)
X_LAG = 0
FINISH_MIB = 60
PIECES = 4
EARLY = 2


def grid(shape):
    return lax.broadcasted_iota(jnp.int32, shape, 0), lax.broadcasted_iota(jnp.int32, shape, 1)


def block_turn():
    row, col = grid((256, 256))
    return ((row & 15) * 16 + (row >> 4) == col).astype(F32).astype(BF)


def output_turn():
    row, col = grid((256, 256))
    m = row >> 2
    stored = (m & 35) + ((m >> 2) & 1) * 16 + ((m >> 3) & 3) * 4
    return ((row & 3) * 64 + stored == col).astype(F32).astype(BF)


def index_table(order, number, stored):
    row, col = grid((128, 128))
    if stored:
        row = (row & 99) + ((row >> 4) & 1) * 4 + ((row >> 2) & 3) * 8
    mapped = jnp.zeros((128, 128), jnp.int32)
    for b in range(7):
        mapped = mapped + (((row >> b) & 1) << order[number, b])
    return (mapped == col).astype(F32)


def dot(a, b):
    return jnp.dot(a, b, preferred_element_type=F32)


def dot_nt(a, b):
    return lax.dot_general(a, b, (((1,), (1,)), ((), ())), preferred_element_type=F32)


def dot_tn(a, b):
    return lax.dot_general(a, b, (((0,), (0,)), ((), ())), preferred_element_type=F32)


def planes_down(a, b):
    top = jnp.concatenate([a[:, :128], b[:, :128]], axis=1)
    low = jnp.concatenate([a[:, 128:], b[:, 128:]], axis=1)
    return jnp.concatenate([top, low], axis=0)


def planes_up(o, which):
    half = o.shape[0] // 2
    lanes = slice(128 * which, 128 * which + 128)
    return jnp.concatenate([o[:half, lanes], o[half:, lanes]], axis=1)


def with_turned(l):
    return jnp.concatenate([l, jnp.concatenate([-l[:, 128:], l[:, :128]], axis=1)], axis=0)


def batches(count, size, load, compute, store):
    def body(i, carry):
        made = [compute(v) for v in [load(i * size + u) for u in range(size)]]
        for u in range(size):
            store(i * size + u, made[u])
        return carry

    lax.fori_loop(0, count // size, body, 0)


def kernel(
    c_in, x_in, bank_in, slices, order,
    sgr, eout,
    craw, xraw, bank, pickers,
    w1f, w1b, w2f, w2b, w3b, w3all, turn,
    csend, xsend, call, xq, b2, b2t, b1t, sg, xt, l1t, l2t, e, rx, ryc, rz, fin,
    in_s, c_ss, c_rs, x_ss, x_rs, loc, g_ss, g_rs, f_ss, f_rs, s_ss, s_rs,
    e1s, e1r, e2s, e2r, e3s, e3r, e4s, e4r, e5s, e5r,
):
    grp, mem = lax.axis_index("grp"), lax.axis_index("mem")
    x, zh = grp // 2, grp % 2
    y, zl, c = mem // 8, (mem // 2) % 4, mem % 2
    z = zh * 4 + zl

    def device(dx, dy, dz, dc):
        x2, y2, z2, c2 = (x + dx) % NX, (y + dy) % NY, (z + dz) % NZ, (c + dc) % NC
        return (x2 * 2 + z2 // 4, (y2 * 4 + z2 % 4) * 2 + c2)

    def yzc(t):
        return t // 16, t % 8, (t // 8) % 2

    loads = [pltpu.make_async_copy(a, b, in_s.at[i]) for i, (a, b) in enumerate(((c_in, craw), (x_in, xraw), (bank_in, bank)))]
    for load in loads:
        load.start()
    bar = pltpu.get_barrier_semaphore()

    def greet(t, carry):
        dy, dz, dc = yzc(t)
        pl.semaphore_signal(bar, inc=1, device_id=device(0, dy, dz, dc), device_id_type=MESH)
        return carry

    lax.fori_loop(1, 64, greet, 0)
    for dx in range(1, NX):
        pl.semaphore_signal(bar, inc=1, device_id=device(dx, 0, 0, 0), device_id_type=MESH)

    def extract(raw, send):
        def load(i):
            mp, rb = i // 8, i % 8
            rows = pl.ds(pl.multiple_of(16 * rb, 16), 16)
            return jnp.concatenate([raw[:, 2 * mp + mm, rows, :].reshape(256, 128) for mm in range(2)], axis=1)

        def store(i, o):
            mp, rb = i // 8, i % 8
            for mm in range(2):
                for r in range(8):
                    for cc in range(2):
                        q = (r * 2 + cc) * 16
                        send[8 * rb + r, 2 * mp + mm, :, cc * 128:cc * 128 + 128] = o[q:q + 16, mm * 128:mm * 128 + 128]

        batches(16, 8, load, lambda v: dot(turn[...], v).astype(BF), store)

    turn[...] = block_turn()
    loads[0].wait()
    extract(craw, csend)
    pl.semaphore_wait(bar, 66)

    def make_gates():
        for s in range(3):
            pickers[s] = index_table(order, s, s == 1)
            small = pickers[s].astype(BF)
            planes, turned = [], []
            for q in range(2):
                chosen = bank[s, slices[s], q]
                planes.append(dot_nt(dot(small, chosen).astype(BF), small).astype(BF))
                turned.append(dot_nt(dot_nt(small, chosen).astype(BF), small).astype(BF))
            whole, flipped = ((w1b, w1f), (w2f, w2b), (None, w3all))[s]
            if whole is not None:
                whole[0:128, 0:128] = planes[0]
                whole[0:128, 128:256] = -planes[1]
                whole[128:256, 0:128] = planes[1]
                whole[128:256, 128:256] = planes[0]
            flipped[0:128, 0:128] = turned[0]
            flipped[0:128, 128:256] = turned[1]
            flipped[128:256, 0:128] = -turned[1]
            flipped[128:256, 128:256] = turned[0]
        at = pl.multiple_of(32 * x, 32)
        w3b[0:32, :] = w3all[pl.ds(at, 32), :]
        w3b[32:64, :] = w3all[pl.ds(128 + at, 32), :]

    m_own = pl.multiple_of(y * 32 + c * 16 + zl * 4, 4)

    def part_of(dy, dz, dc):
        s = (z + dz + 6) % NZ
        return 2 * ((((y + dy) % NY) * 4 + s % 4) * 2 + (c + dc) % NC) + s // 4

    def c_copy(t):
        dy, dz, dc = yzc(t)
        return pltpu.make_async_remote_copy(
            src_ref=csend.at[part_of(dy, dz, dc)],
            dst_ref=call.at[grp, pl.ds(m_own, 4)],
            send_sem=c_ss.at[t], recv_sem=c_rs.at[t],
            device_id=device(0, dy, dz, dc), device_id_type=MESH)

    def x_copy(t):
        dy, dz, dc = yzc(t)
        return pltpu.make_async_remote_copy(
            src_ref=xsend.at[part_of(dy, dz, dc)],
            dst_ref=xq.at[zh, pl.ds(m_own, 4)],
            send_sem=x_ss.at[t], recv_sem=x_rs.at[t],
            device_id=device(0, dy, dz, dc), device_id_type=MESH)

    own_c = pltpu.make_async_copy(csend.at[part_of(0, 0, 0)], call.at[grp, pl.ds(m_own, 4)], loc.at[0])
    own_x = pltpu.make_async_copy(xsend.at[part_of(0, 0, 0)], xq.at[zh, pl.ds(m_own, 4)], loc.at[1])

    def start_group(copy, g):
        for dz in Z_ORDER:
            if dz == 0:
                @pl.when(g > 0)
                def _():
                    copy(g * 8).start()
            else:
                copy(g * 8 + dz).start()

    def c_start(g, carry):
        start_group(c_copy, g)
        return carry

    def x_start(g, carry):
        start_group(x_copy, g)
        return carry

    own_c.start()
    lax.fori_loop(0, 8, c_start, 0)
    loads[1].wait()
    extract(xraw, xsend)
    own_x.start()
    if X_LAG < 0:
        lax.fori_loop(0, 8, x_start, 0)
    loads[2].wait()
    make_gates()

    def m_of(g):
        dy, dc = g // 2, g % 2
        return pl.multiple_of(((y + NY - dy) % NY) * 32 + ((c + NC - dc) % NC) * 16, 16)

    def near(g, way):
        part = call.at[pl.ds(2 * x, 2), pl.ds(m_of(g), 16)]
        return pltpu.make_async_remote_copy(
            src_ref=part, dst_ref=part, send_sem=g_ss.at[way, g], recv_sem=g_rs.at[way, g],
            device_id=device(1 if way == 0 else NX - 1, 0, 0, 0), device_id_type=MESH)

    def far(g, way):
        owner = (x + NX - 1) % NX if way == 0 else (x + 1) % NX
        part = call.at[pl.ds(2 * owner, 2), pl.ds(m_of(g) + 8 * way, 8)]
        return pltpu.make_async_remote_copy(
            src_ref=part, dst_ref=part, send_sem=f_ss.at[way, g], recv_sem=f_rs.at[way, g],
            device_id=device(1 if way == 0 else NX - 1, 0, 0, 0), device_id_type=MESH)

    def relay(g):
        for way in range(2):
            near(g, way).wait_recv()
            far(g, way).start()

    def arrive(g, carry):
        for dz in Z_ORDER:
            if dz == 0:
                @pl.when(g > 0)
                def _():
                    c_copy(g * 8).wait_recv()
            else:
                c_copy(g * 8 + dz).wait_recv()

        @pl.when(g == 0)
        def _():
            own_c.wait()

        near(g, 0).start()
        near(g, 1).start()

        if X_LAG >= 0:
            @pl.when(g >= X_LAG)
            def _():
                start_group(x_copy, g - X_LAG)

        @pl.when(g >= 1)
        def _():
            relay(g - 1)

        return carry

    lax.fori_loop(0, 8, arrive, 0)
    if X_LAG > 0:
        lax.fori_loop(8 - X_LAG, 8, x_start, 0)
    relay(7)

    def all_n(m):
        return call[:, m].reshape(128, 256)

    def third(g, carry):
        far(g, 0).wait_recv()
        far(g, 1).wait_recv()

        base = m_of(g)
        made = [planes_down(all_n(base + 2 * p), all_n(base + 2 * p + 1)) for p in range(8)]
        made = [dot(w3b[...], v).astype(BF) for v in made]
        for p in range(8):
            b2[base + 2 * p] = planes_up(made[p], 0)
            b2[base + 2 * p + 1] = planes_up(made[p], 1)
        return carry

    lax.fori_loop(0, 8, third, 0)

    def turn_all(src, dst, to_rows):
        def places(i):
            return pl.ds(pl.multiple_of(16 * (i % 8), 16), 16), pl.ds(pl.multiple_of(16 * (i // 8), 16), 16)

        def load(i):
            m, n = places(i)
            if len(src.shape) == 4:
                return src[i // 8, m].reshape(256, 256)
            return (src[m, n, :] if to_rows else src[n, m, :]).reshape(256, 256)

        def store(i, o):
            m, n = places(i)
            if to_rows:
                dst[n, m, :] = o.reshape(16, 16, 256)
            else:
                dst[m, n, :] = o.reshape(16, 16, 256)

        batches(16, 8, load, lambda v: dot(turn[...], v).astype(BF), store)

    def gate_two(src, dst, w, base, pairs):
        def store(i, o):
            dst[base + 2 * i] = planes_up(o, 0)
            dst[base + 2 * i + 1] = planes_up(o, 1)

        batches(pairs, 4, lambda i: planes_down(src[base + 2 * i], src[base + 2 * i + 1]),
                lambda v: dot(w[...], v).astype(BF), store)

    def gate_one(src, dst, w, base, pairs):
        def store(i, o):
            dst[pl.ds(base + 2 * i, 2)] = o.reshape(2, 128, 256)

        batches(pairs, 4, lambda i: src[pl.ds(base + 2 * i, 2)].reshape(256, 256),
                lambda v: dot(v, w[...]).astype(BF), store)

    s_here = (z + 6) % NZ
    part_here = s_here // 4

    per = 16 // PIECES

    def back(half, k):
        z_to = 4 * half + s_here % 4
        return pltpu.make_async_remote_copy(
            src_ref=sg.at[pl.ds(16 * half + per * k, per)], dst_ref=sgr.at[part_here, pl.ds(per * k, per)],
            send_sem=s_ss.at[half, k], recv_sem=s_rs.at[part_here, k],
            device_id=device(0, 0, z_to + NZ - z, 0), device_id_type=MESH)

    turn_all(b2, b2t, True)
    for k in range(2):
        for half in range(2):
            n = 16 * half + 8 * k
            gate_two(b2t, b1t, w2b, n, 4)
            gate_one(b1t, sg, w1b, n, 4)
        for j in range(PIECES // 2 * k, PIECES // 2 * (k + 1)):
            if j < EARLY:
                back(0, j).start()
                back(1, j).start()

    def x_arrive(t, carry):
        x_copy(t).wait_recv()
        return carry

    own_x.wait()
    lax.fori_loop(1, 64, x_arrive, 0)

    turn_all(xq, xt, True)
    gate_one(xt, l1t, w1f, 0, 16)
    gate_two(l1t, l2t, w2f, 0, 16)
    turn_all(l2t, b2, False)

    def grad_two(i, acc):
        for u in range(8):
            acc = acc + dot_nt(b2t[8 * i + u], with_turned(l1t[8 * i + u]))
        return acc

    acc = lax.fori_loop(0, 4, grad_two, jnp.zeros((128, 256), F32))
    e[256:384, :] = acc[:, :128]
    e[384:512, :] = acc[:, 128:]

    def grad_one(i, acc):
        rows = pl.ds(8 * i, 8)
        return acc + dot_tn(b1t[rows].reshape(1024, 256), xt[rows].reshape(1024, 256))

    acc = lax.fori_loop(0, 4, grad_one, jnp.zeros((256, 256), F32))
    e[0:128, :] = acc[0:128, 0:128] + acc[128:256, 128:256]
    e[128:256, :] = acc[128:256, 0:128] - acc[0:128, 128:256]

    def grad_three(i, acc):
        for p in range(16):
            acc = acc + dot_nt(all_n(16 * i + p), with_turned(b2[16 * i + p]))
        return acc

    acc3 = lax.fori_loop(0, 8, grad_three, jnp.zeros((128, 64), F32))
    acc3 = jnp.transpose(jnp.concatenate([acc3, jnp.zeros((128, 64), F32)], axis=1))
    e[512:768, :] = jnp.zeros((256, 128), F32)
    spot = pl.multiple_of(32 * x, 32)
    e[pl.ds(512 + spot, 32), :] = acc3[0:32, :]
    e[pl.ds(640 + spot, 32), :] = acc3[32:64, :]

    def one(dx):
        to = (x + dx) % NX
        return pltpu.make_async_remote_copy(
            src_ref=e.at[pl.ds(pl.multiple_of(192 * to, 192), 192), :], dst_ref=rx.at[x],
            send_sem=e1s.at[dx], recv_sem=e1r.at[dx], device_id=device(dx, 0, 0, 0), device_id_type=MESH)

    def yc(k):
        return ((y + k // 2) % NY) * 2 + (c + k % 2) % NC

    def two(k):
        to = yc(k)
        return pltpu.make_async_remote_copy(
            src_ref=ryc.at[8, pl.ds(pl.multiple_of(24 * to, 8), 24), :],
            dst_ref=ryc.at[y * 2 + c, pl.ds(0, 24), :],
            send_sem=e2s.at[k], recv_sem=e2r.at[k], device_id=device(0, k // 2, 0, k % 2), device_id_type=MESH)

    def three(dz):
        return pltpu.make_async_remote_copy(
            src_ref=rz.at[z], dst_ref=rz.at[z],
            send_sem=e3s.at[dz], recv_sem=e3r.at[dz], device_id=device(0, 0, dz, 0), device_id_type=MESH)

    def four(k):
        rows = fin.at[pl.ds(pl.multiple_of(192 * x + 24 * (y * 2 + c), 8), 24), :]
        return pltpu.make_async_remote_copy(
            src_ref=rows, dst_ref=rows,
            send_sem=e4s.at[k], recv_sem=e4r.at[k], device_id=device(0, k // 2, 0, k % 2), device_id_type=MESH)

    def five(dx):
        rows = fin.at[pl.ds(pl.multiple_of(192 * x, 192), 192), :]
        return pltpu.make_async_remote_copy(
            src_ref=rows, dst_ref=rows,
            send_sem=e5s.at[dx], recv_sem=e5r.at[dx], device_id=device(dx, 0, 0, 0), device_id_type=MESH)

    for dx in range(1, NX):
        one(dx).start()
    rx[x] = e[pl.ds(pl.multiple_of(192 * x, 192), 192), :]
    for dx in range(1, NX):
        one(dx).wait_recv()
    ryc[8] = (rx[0] + rx[1]) + (rx[2] + rx[3])
    for k in range(1, 8):
        two(k).start()
    ryc[y * 2 + c, 0:24, :] = ryc[8, pl.ds(pl.multiple_of(24 * (y * 2 + c), 8), 24), :]
    for k in range(1, 8):
        two(k).wait_recv()
    total = ryc[0, 0:24, :]
    for k in range(1, 8):
        total = total + ryc[k, 0:24, :]
    rz[z] = total
    for dz in range(1, NZ):
        three(dz).start()
    for j in range(EARLY, PIECES):
        back(0, j).start()
        back(1, j).start()
    for dz in range(1, NZ):
        three(dz).wait_recv()
    total = rz[0]
    for k in range(1, NZ):
        total = total + rz[k]
    fin[pl.ds(pl.multiple_of(192 * x + 24 * (y * 2 + c), 8), 24), :] = total
    for k in range(1, 8):
        four(k).start()
    for k in range(1, 8):
        four(k).wait_recv()
    for dx in range(1, NX):
        five(dx).start()
    for dx in range(1, NX):
        five(dx).wait_recv()

    def exact(a, b, dims):
        return lax.dot_general(a, b, (dims, ((), ())), precision=HIGH, preferred_element_type=F32)

    factor = 1.0 / (128 * 64**0.5)
    sides = [(s, q) for s in range(3) for q in range(2)]
    moved = [exact(pickers[s], fin[256 * s + 128 * q:256 * s + 128 * q + 128, :], ((0,), (1,) if s == 2 else (0,))) for s, q in sides]
    for (s, q), part in zip(sides, moved):
        eout[s, q] = exact(part, pickers[s], ((1,), (0,))) * factor

    def c_gone(t, carry):
        c_copy(t).wait_send()
        x_copy(t).wait_send()
        return carry

    lax.fori_loop(1, 64, c_gone, 0)

    def g_gone(g, carry):
        for way in range(2):
            near(g, way).wait_send()
            far(g, way).wait_send()
        return carry

    lax.fori_loop(0, 8, g_gone, 0)
    for dx in range(1, NX):
        one(dx).wait_send()
        five(dx).wait_send()
    for k in range(1, 8):
        two(k).wait_send()
        three(k).wait_send()
        four(k).wait_send()

    def landed(part, k):
        return pltpu.make_async_remote_copy(
            src_ref=sg.at[pl.ds(0, per)], dst_ref=sgr.at[part, pl.ds(per * k, per)],
            send_sem=s_ss.at[0, k], recv_sem=s_rs.at[part, k],
            device_id=device(0, 0, 2, 0), device_id_type=MESH)

    for k in range(PIECES):
        for half in range(2):
            landed(half, k).wait_recv()
            back(half, k).wait_send()


def finish(sgr, sums, out, eout, outturn):
    @pl.when(pl.program_id(0) == 0)
    def _():
        outturn[...] = output_turn()
        eout[...] = sums[...]

    made = []
    for i in range(4):
        n, rows = 2 * (i // 2), slice(64 * (i % 2), 64 * (i % 2) + 64)
        sides = [jnp.concatenate([sgr[r, n + nn, rows, cc * 128:cc * 128 + 128] for r in range(2) for cc in range(2)], axis=0)
                 for nn in range(2)]
        made.append(dot(outturn[...], jnp.concatenate(sides, axis=1)).astype(BF))
    for i in range(4):
        n, at = 2 * (i // 2), slice(256 * (i % 2), 256 * (i % 2) + 256)
        out[n, at, :] = made[i][:, :128]
        out[n + 1, at, :] = made[i][:, 128:]


def local(initial_state, cotangent, gate_bank, slice_index, mode_order):
    hbm = pl.BlockSpec(memory_space=pl.ANY)
    vm = pl.BlockSpec(memory_space=pltpu.VMEM)
    sm = pl.BlockSpec(memory_space=pltpu.SMEM)
    big = lambda *shape: pltpu.VMEM(shape, BF)
    wide = lambda *shape: pltpu.VMEM(shape, F32)
    sem = lambda *shape: pltpu.SemaphoreType.DMA(shape)
    backs, sums = pl.pallas_call(
        kernel,
        out_shape=(jax.ShapeDtypeStruct((2, 16, 128, 256), BF), jax.ShapeDtypeStruct((3, 2, 128, 128), F32)),
        in_specs=[hbm, hbm, hbm, sm, sm],
        out_specs=(hbm, vm),
        scratch_shapes=[
            big(16, 4, 128, 128), big(16, 4, 128, 128), big(3, 4, 2, 128, 128), wide(3, 128, 128),
            big(256, 256), big(256, 256), big(256, 256), big(256, 256), big(64, 256), big(256, 256), big(256, 256),
            big(64, 4, 16, 256), big(64, 4, 16, 256), big(8, 128, 16, 256), big(2, 128, 16, 256),
            big(128, 32, 256), big(32, 128, 256), big(32, 128, 256), big(32, 128, 256),
            big(32, 128, 256), big(32, 128, 256), big(32, 128, 256),
            wide(768, 128), wide(4, 192, 128), wide(9, 192, 128), wide(8, 24, 128), wide(768, 128),
            sem(3), sem(64), sem(64), sem(64), sem(64), sem(2), sem(2, 8), sem(2, 8), sem(2, 8), sem(2, 8), sem(2, PIECES), sem(2, PIECES),
            sem(4), sem(4), sem(8), sem(8), sem(8), sem(8), sem(8), sem(8), sem(4), sem(4),
        ],
        compiler_params=pltpu.CompilerParams(collective_id=0, has_side_effects=True, vmem_limit_bytes=54 << 20),
        name="gradients",
    )(
        cotangent.reshape(16, 4, 128, 128), initial_state.reshape(16, 4, 128, 128),
        gate_bank, slice_index, mode_order,
    )
    out, grads = pl.pallas_call(
        finish,
        grid=(4,),
        out_shape=(jax.ShapeDtypeStruct((16, 512, 128), BF), jax.ShapeDtypeStruct((3, 2, 128, 128), F32)),
        in_specs=[
            pl.BlockSpec((2, 4, 128, 256), lambda i: (0, i, 0, 0)),
            pl.BlockSpec((3, 2, 128, 128), lambda i: (0, 0, 0, 0)),
        ],
        out_specs=(pl.BlockSpec((4, 512, 128), lambda i: (i, 0, 0)), pl.BlockSpec((3, 2, 128, 128), lambda i: (0, 0, 0, 0))),
        scratch_shapes=[big(256, 256)],
        compiler_params=pltpu.CompilerParams(vmem_limit_bytes=FINISH_MIB << 20),
        name="outputs",
    )(backs, sums)
    return grads, out.reshape(16, 128, 2, 2, 128)


def solution(mesh):
    in_specs = (P("grp", "mem", None, None, None), P("grp", "mem", None, None, None), P(), P(), P())
    out_specs = (P(), P("grp", None, "mem", None, None))
    return jax.shard_map(local, mesh=mesh, in_specs=in_specs, out_specs=out_specs, check_vma=False)
```

```python
import jax
import jax.numpy as jnp
from jax import lax
from jax.experimental import pallas as pl
from jax.experimental.pallas import tpu as pltpu
from jax.sharding import PartitionSpec as P

MESH = pl.DeviceIdType.MESH
BF = jnp.bfloat16
F32 = jnp.float32
HIGH = lax.Precision.HIGHEST
NX, NY, NZ, NC = 4, 4, 8, 2
Z_ORDER = (4, 3, 5, 2, 6, 1, 7, 0)
PIECES = 8
EARLY = 5
STEPS = 2


def grid(shape):
    return lax.broadcasted_iota(jnp.int32, shape, 0), lax.broadcasted_iota(jnp.int32, shape, 1)


def block_turn():
    row, col = grid((256, 256))
    return ((row & 15) * 16 + (row >> 4) == col).astype(F32).astype(BF)


def output_turn():
    row, col = grid((256, 256))
    m = row >> 2
    stored = (m & 35) + ((m >> 2) & 1) * 16 + ((m >> 3) & 3) * 4
    return ((row & 3) * 64 + stored == col).astype(F32).astype(BF)


def index_table(order, number, stored):
    row, col = grid((128, 128))
    if stored:
        row = (row & 99) + ((row >> 4) & 1) * 4 + ((row >> 2) & 3) * 8
    mapped = jnp.zeros((128, 128), jnp.int32)
    for b in range(7):
        mapped = mapped + (((row >> b) & 1) << order[number, b])
    return (mapped == col).astype(F32)


def dot(a, b):
    return jnp.dot(a, b, preferred_element_type=F32)


def dot_nt(a, b):
    return lax.dot_general(a, b, (((1,), (1,)), ((), ())), preferred_element_type=F32)


def dot_tn(a, b):
    return lax.dot_general(a, b, (((0,), (0,)), ((), ())), preferred_element_type=F32)


def planes_down(a, b):
    top = jnp.concatenate([a[:, :128], b[:, :128]], axis=1)
    low = jnp.concatenate([a[:, 128:], b[:, 128:]], axis=1)
    return jnp.concatenate([top, low], axis=0)


def planes_up(o, which):
    half = o.shape[0] // 2
    lanes = slice(128 * which, 128 * which + 128)
    return jnp.concatenate([o[:half, lanes], o[half:, lanes]], axis=1)


def with_turned(l):
    return jnp.concatenate([l, jnp.concatenate([-l[:, 128:], l[:, :128]], axis=1)], axis=0)


def batches(count, size, load, compute, store):
    def body(i, carry):
        made = [compute(v) for v in [load(i * size + u) for u in range(size)]]
        for u in range(size):
            store(i * size + u, made[u])
        return carry

    lax.fori_loop(0, count // size, body, 0)


def kernel(
    c_in, x_in, bank_in, slices, order,
    sgr, eout,
    craw, xraw, bank, pickers,
    w1f, w1b, w2f, w2b, w3b, w3all, turn,
    csend, xsend, call, xq, b2, b2t, b1t, sg, xt, l1t, l2t, e, rx, ryc, rz, fin,
    in_s, c_ss, c_rs, x_ss, x_rs, loc, g_ss, g_rs, f_ss, f_rs, s_ss, s_rs,
    e1s, e1r, e2s, e2r, e3s, e3r, e4s, e4r, e5s, e5r,
):
    grp, mem = lax.axis_index("grp"), lax.axis_index("mem")
    x, zh = grp // 2, grp % 2
    y, zl, c = mem // 8, (mem // 2) % 4, mem % 2
    z = zh * 4 + zl

    def device(dx, dy, dz, dc):
        x2, y2, z2, c2 = (x + dx) % NX, (y + dy) % NY, (z + dz) % NZ, (c + dc) % NC
        return (x2 * 2 + z2 // 4, (y2 * 4 + z2 % 4) * 2 + c2)

    def yzc(t):
        return t // 16, t % 8, (t // 8) % 2

    loads = [pltpu.make_async_copy(a, b, in_s.at[i]) for i, (a, b) in enumerate(((c_in, craw), (x_in, xraw), (bank_in, bank)))]
    for load in loads:
        load.start()
    bar = pltpu.get_barrier_semaphore()

    def greet(t, carry):
        dy, dz, dc = yzc(t)
        pl.semaphore_signal(bar, inc=1, device_id=device(0, dy, dz, dc), device_id_type=MESH)
        return carry

    lax.fori_loop(1, 64, greet, 0)
    for dx in range(1, NX):
        pl.semaphore_signal(bar, inc=1, device_id=device(dx, 0, 0, 0), device_id_type=MESH)

    def extract(raw, send, dy):
        first = 2 * ((y + dy) % NY)
        loaded = []
        for i in range(4):
            mp, rows = i // 2, pl.ds(pl.multiple_of(16 * (first + i % 2), 16), 16)
            loaded.append(jnp.concatenate([raw[:, 2 * mp + mm, rows, :].reshape(256, 128) for mm in range(2)], axis=1))
        made = [dot(turn[...], v).astype(BF) for v in loaded]
        for i in range(4):
            mp, r0 = i // 2, 8 * (first + i % 2)
            for mm in range(2):
                for r in range(8):
                    for cc in range(2):
                        q = (r * 2 + cc) * 16
                        send[r0 + r, 2 * mp + mm, :, cc * 128:cc * 128 + 128] = made[i][q:q + 16, mm * 128:mm * 128 + 128]

    turn[...] = block_turn()
    loads[0].wait()
    extract(craw, csend, 0)
    pl.semaphore_wait(bar, 66)

    def make_gates():
        for s in range(3):
            pickers[s] = index_table(order, s, s == 1)
            small = pickers[s].astype(BF)
            planes, turned = [], []
            for q in range(2):
                chosen = bank[s, slices[s], q]
                planes.append(dot_nt(dot(small, chosen).astype(BF), small).astype(BF))
                turned.append(dot_nt(dot_nt(small, chosen).astype(BF), small).astype(BF))
            whole, flipped = ((w1b, w1f), (w2f, w2b), (None, w3all))[s]
            if whole is not None:
                whole[0:128, 0:128] = planes[0]
                whole[0:128, 128:256] = -planes[1]
                whole[128:256, 0:128] = planes[1]
                whole[128:256, 128:256] = planes[0]
            flipped[0:128, 0:128] = turned[0]
            flipped[0:128, 128:256] = turned[1]
            flipped[128:256, 0:128] = -turned[1]
            flipped[128:256, 128:256] = turned[0]
        at = pl.multiple_of(32 * x, 32)
        w3b[0:32, :] = w3all[pl.ds(at, 32), :]
        w3b[32:64, :] = w3all[pl.ds(128 + at, 32), :]

    m_own = pl.multiple_of(y * 32 + c * 16 + zl * 4, 4)

    def part_of(dy, dz, dc):
        s = (z + dz + 6) % NZ
        return 2 * ((((y + dy) % NY) * 4 + s % 4) * 2 + (c + dc) % NC) + s // 4

    def c_copy(t):
        dy, dz, dc = yzc(t)
        return pltpu.make_async_remote_copy(
            src_ref=csend.at[part_of(dy, dz, dc)],
            dst_ref=call.at[grp, pl.ds(m_own, 4)],
            send_sem=c_ss.at[t], recv_sem=c_rs.at[t],
            device_id=device(0, dy, dz, dc), device_id_type=MESH)

    def x_copy(t):
        dy, dz, dc = yzc(t)
        return pltpu.make_async_remote_copy(
            src_ref=xsend.at[part_of(dy, dz, dc)],
            dst_ref=xq.at[zh, pl.ds(m_own, 4)],
            send_sem=x_ss.at[t], recv_sem=x_rs.at[t],
            device_id=device(0, dy, dz, dc), device_id_type=MESH)

    own_c = pltpu.make_async_copy(csend.at[part_of(0, 0, 0)], call.at[grp, pl.ds(m_own, 4)], loc.at[0])
    own_x = pltpu.make_async_copy(xsend.at[part_of(0, 0, 0)], xq.at[zh, pl.ds(m_own, 4)], loc.at[1])

    def start_group(copy, g):
        for dz in Z_ORDER:
            if dz == 0:
                @pl.when(g > 0)
                def _():
                    copy(g * 8).start()
            else:
                copy(g * 8 + dz).start()

    own_c.start()
    start_group(c_copy, 0)
    start_group(c_copy, 1)

    def c_start(dy, carry):
        extract(craw, csend, dy)
        start_group(c_copy, 2 * dy)
        start_group(c_copy, 2 * dy + 1)
        return carry

    lax.fori_loop(1, 4, c_start, 0)
    loads[1].wait()

    def x_ready(dy, carry):
        extract(xraw, xsend, dy)
        return carry

    lax.fori_loop(0, 4, x_ready, 0)
    own_x.start()
    loads[2].wait()
    make_gates()

    def m_of(g):
        dy, dc = g // 2, g % 2
        return pl.multiple_of(((y + NY - dy) % NY) * 32 + ((c + NC - dc) % NC) * 16, 16)

    def near(g, way):
        part = call.at[pl.ds(2 * x, 2), pl.ds(m_of(g), 16)]
        return pltpu.make_async_remote_copy(
            src_ref=part, dst_ref=part, send_sem=g_ss.at[way, g], recv_sem=g_rs.at[way, g],
            device_id=device(1 if way == 0 else NX - 1, 0, 0, 0), device_id_type=MESH)

    def far(g, way):
        owner = (x + NX - 1) % NX if way == 0 else (x + 1) % NX
        part = call.at[pl.ds(2 * owner, 2), pl.ds(m_of(g) + 8 * way, 8)]
        return pltpu.make_async_remote_copy(
            src_ref=part, dst_ref=part, send_sem=f_ss.at[way, g], recv_sem=f_rs.at[way, g],
            device_id=device(1 if way == 0 else NX - 1, 0, 0, 0), device_id_type=MESH)

    def relay(g):
        for way in range(2):
            near(g, way).wait_recv()
            far(g, way).start()

    def arrive(g, carry):
        for dz in Z_ORDER:
            if dz == 0:
                @pl.when(g > 0)
                def _():
                    c_copy(g * 8).wait_recv()
            else:
                c_copy(g * 8 + dz).wait_recv()

        @pl.when(g == 0)
        def _():
            own_c.wait()

        near(g, 0).start()
        near(g, 1).start()

        start_group(x_copy, g)

        @pl.when(g >= 1)
        def _():
            relay(g - 1)

        return carry

    lax.fori_loop(0, 8, arrive, 0)
    relay(7)

    def all_n(m):
        return call[:, m].reshape(128, 256)

    def third(g, carry):
        far(g, 0).wait_recv()
        far(g, 1).wait_recv()

        base = m_of(g)
        made = [planes_down(all_n(base + 2 * p), all_n(base + 2 * p + 1)) for p in range(8)]
        made = [dot(w3b[...], v).astype(BF) for v in made]
        for p in range(8):
            b2[base + 2 * p] = planes_up(made[p], 0)
            b2[base + 2 * p + 1] = planes_up(made[p], 1)
        return carry

    lax.fori_loop(0, 8, third, 0)

    def turn_all(src, dst, to_rows):
        def places(i):
            return pl.ds(pl.multiple_of(16 * (i % 8), 16), 16), pl.ds(pl.multiple_of(16 * (i // 8), 16), 16)

        def load(i):
            m, n = places(i)
            if len(src.shape) == 4:
                return src[i // 8, m].reshape(256, 256)
            return (src[m, n, :] if to_rows else src[n, m, :]).reshape(256, 256)

        def store(i, o):
            m, n = places(i)
            if to_rows:
                dst[n, m, :] = o.reshape(16, 16, 256)
            else:
                dst[m, n, :] = o.reshape(16, 16, 256)

        batches(16, 8, load, lambda v: dot(turn[...], v).astype(BF), store)

    def gate_two(src, dst, w, base, pairs):
        def store(i, o):
            dst[base + 2 * i] = planes_up(o, 0)
            dst[base + 2 * i + 1] = planes_up(o, 1)

        batches(pairs, 4, lambda i: planes_down(src[base + 2 * i], src[base + 2 * i + 1]),
                lambda v: dot(w[...], v).astype(BF), store)

    def gate_one(src, dst, w, base, pairs):
        def store(i, o):
            dst[pl.ds(base + 2 * i, 2)] = o.reshape(2, 128, 256)

        batches(pairs, 4, lambda i: src[pl.ds(base + 2 * i, 2)].reshape(256, 256),
                lambda v: dot(v, w[...]).astype(BF), store)

    s_here = (z + 6) % NZ
    part_here = s_here // 4

    per = 16 // PIECES

    def back(half, k):
        z_to = 4 * half + s_here % 4
        return pltpu.make_async_remote_copy(
            src_ref=sg.at[pl.ds(16 * half + per * k, per)], dst_ref=sgr.at[part_here, pl.ds(per * k, per)],
            send_sem=s_ss.at[half, k], recv_sem=s_rs.at[part_here, k],
            device_id=device(0, 0, z_to + NZ - z, 0), device_id_type=MESH)

    turn_all(b2, b2t, True)
    for k in range(2):
        for half in range(2):
            n = 16 * half + 8 * k
            gate_two(b2t, b1t, w2b, n, 4)
            gate_one(b1t, sg, w1b, n, 4)
        for j in range(PIECES // 2 * k, PIECES // 2 * (k + 1)):
            if j < EARLY:
                back(0, j).start()
                back(1, j).start()

    def x_arrive(t, carry):
        x_copy(t).wait_recv()
        return carry

    own_x.wait()
    lax.fori_loop(1, 64, x_arrive, 0)

    turn_all(xq, xt, True)
    gate_one(xt, l1t, w1f, 0, 16)

    def grad_two(i, acc):
        for u in range(8):
            acc = acc + dot_nt(b2t[8 * i + u], with_turned(l1t[8 * i + u]))
        return acc

    acc = lax.fori_loop(0, 4, grad_two, jnp.zeros((128, 256), F32))
    for k in range(NX):
        e[k, 64:128, :] = acc[64 * (k % 2):64 * (k % 2) + 64, 128 * (k // 2):128 * (k // 2) + 128]

    def grad_one(i, acc):
        rows = pl.ds(8 * i, 8)
        return acc + dot_tn(b1t[rows].reshape(1024, 256), xt[rows].reshape(1024, 256))

    acc = lax.fori_loop(0, 4, grad_one, jnp.zeros((256, 256), F32))
    for k in range(2):
        i = slice(64 * k, 64 * k + 64)
        j = slice(128 + 64 * k, 128 + 64 * k + 64)
        e[k, 0:64, :] = acc[i, 0:128] + acc[j, 128:256]
        e[2 + k, 0:64, :] = acc[j, 0:128] - acc[i, 128:256]

    def one(dx):
        to = (x + dx) % NX
        return pltpu.make_async_remote_copy(
            src_ref=e.at[to], dst_ref=rx.at[x],
            send_sem=e1s.at[dx], recv_sem=e1r.at[dx], device_id=device(dx, 0, 0, 0), device_id_type=MESH)

    for dx in range(1, NX):
        one(dx).start()
    rx[x] = e[x]

    gate_two(l1t, l2t, w2f, 0, 16)
    turn_all(l2t, b2, False)

    def grad_three(i, acc):
        for p in range(16):
            acc = acc + dot_nt(all_n(16 * i + p), with_turned(b2[16 * i + p]))
        return acc

    acc = lax.fori_loop(0, 8, grad_three, jnp.zeros((128, 64), F32))
    ryc[8, 128:192, :] = jnp.transpose(jnp.concatenate([acc, jnp.zeros((128, 64), F32)], axis=1))[0:64, :]

    def yc(k):
        return ((y + k // 2) % NY) * 2 + (c + k % 2) % NC

    def two(k):
        to = yc(k)
        return pltpu.make_async_remote_copy(
            src_ref=ryc.at[8, pl.ds(pl.multiple_of(24 * to, 8), 24), :],
            dst_ref=ryc.at[y * 2 + c, pl.ds(0, 24), :],
            send_sem=e2s.at[k], recv_sem=e2r.at[k], device_id=device(0, k // 2, 0, k % 2), device_id_type=MESH)

    def three(dz):
        return pltpu.make_async_remote_copy(
            src_ref=rz.at[z], dst_ref=rz.at[z],
            send_sem=e3s.at[dz], recv_sem=e3r.at[dz], device_id=device(0, 0, dz, 0), device_id_type=MESH)

    def four(k):
        rows = fin.at[x, pl.ds(pl.multiple_of(24 * (y * 2 + c), 8), 24), :]
        return pltpu.make_async_remote_copy(
            src_ref=rows, dst_ref=rows,
            send_sem=e4s.at[k], recv_sem=e4r.at[k], device_id=device(0, k // 2, 0, k % 2), device_id_type=MESH)

    def five(dx):
        rows = fin.at[x]
        return pltpu.make_async_remote_copy(
            src_ref=rows, dst_ref=rows,
            send_sem=e5s.at[dx], recv_sem=e5r.at[dx], device_id=device(dx, 0, 0, 0), device_id_type=MESH)

    for dx in range(1, NX):
        one(dx).wait_recv()
    ryc[8, 0:128, :] = (rx[0] + rx[1]) + (rx[2] + rx[3])
    for k in range(1, 8):
        two(k).start()
    ryc[y * 2 + c, 0:24, :] = ryc[8, pl.ds(pl.multiple_of(24 * (y * 2 + c), 8), 24), :]
    for k in range(1, 8):
        two(k).wait_recv()
    total = ryc[0, 0:24, :]
    for k in range(1, 8):
        total = total + ryc[k, 0:24, :]
    rz[z] = total
    for dz in range(1, NZ):
        three(dz).start()
    for j in range(EARLY, PIECES):
        back(0, j).start()
        back(1, j).start()
    for dz in range(1, NZ):
        three(dz).wait_recv()
    total = rz[0]
    for k in range(1, NZ):
        total = total + rz[k]
    fin[x, pl.ds(pl.multiple_of(24 * (y * 2 + c), 8), 24), :] = total
    for k in range(1, 8):
        four(k).start()
    for k in range(1, 8):
        four(k).wait_recv()
    for dx in range(1, NX):
        five(dx).start()
    for dx in range(1, NX):
        five(dx).wait_recv()

    def exact(a, b, dims):
        return lax.dot_general(a, b, (dims, ((), ())), precision=HIGH, preferred_element_type=F32)

    factor = 1.0 / (128 * 64**0.5)
    sides = [(s, q) for s in range(3) for q in range(2)]

    def sums(s, q):
        if s < 2:
            return jnp.concatenate([fin[2 * q + k, 64 * s:64 * s + 64, :] for k in range(2)], axis=0)
        return jnp.concatenate([fin[k, 128 + 32 * q:160 + 32 * q, :] for k in range(NX)], axis=0)

    moved = [exact(pickers[s], sums(s, q), ((0,), (1,) if s == 2 else (0,))) for s, q in sides]
    for (s, q), part in zip(sides, moved):
        eout[s, q] = exact(part, pickers[s], ((1,), (0,))) * factor

    def c_gone(t, carry):
        c_copy(t).wait_send()
        x_copy(t).wait_send()
        return carry

    lax.fori_loop(1, 64, c_gone, 0)

    def g_gone(g, carry):
        for way in range(2):
            near(g, way).wait_send()
            far(g, way).wait_send()
        return carry

    lax.fori_loop(0, 8, g_gone, 0)
    for dx in range(1, NX):
        one(dx).wait_send()
        five(dx).wait_send()
    for k in range(1, 8):
        two(k).wait_send()
        three(k).wait_send()
        four(k).wait_send()

    def landed(part, k):
        return pltpu.make_async_remote_copy(
            src_ref=sg.at[pl.ds(0, per)], dst_ref=sgr.at[part, pl.ds(per * k, per)],
            send_sem=s_ss.at[0, k], recv_sem=s_rs.at[part, k],
            device_id=device(0, 0, 2, 0), device_id_type=MESH)

    for k in range(PIECES):
        for half in range(2):
            landed(half, k).wait_recv()
            back(half, k).wait_send()


def finish(back, sums, out, eout, outturn, sgr, given, held, in_s, out_s):
    per = 16 // STEPS
    come = pltpu.make_async_copy(sums, held, in_s.at[STEPS])
    go = pltpu.make_async_copy(held, eout, out_s.at[STEPS])

    def load(k):
        at = pl.ds(per * k, per)
        return pltpu.make_async_copy(back.at[:, at], sgr.at[:, at], in_s.at[k])

    def give(k):
        at = pl.ds(per * k, per)
        return pltpu.make_async_copy(given.at[at], out.at[at], out_s.at[k])

    for k in range(STEPS):
        load(k).start()
    come.start()
    outturn[...] = output_turn()
    for k in range(STEPS):
        load(k).wait()
        made = []
        for i in range(per):
            n, rows = per * k + 2 * (i // 2), slice(64 * (i % 2), 64 * (i % 2) + 64)
            sides = [jnp.concatenate([sgr[r, n + nn, rows, cc * 128:cc * 128 + 128] for r in range(2) for cc in range(2)], axis=0)
                     for nn in range(2)]
            made.append(dot(outturn[...], jnp.concatenate(sides, axis=1)).astype(BF))
        for i in range(per):
            n, at = per * k + 2 * (i // 2), slice(256 * (i % 2), 256 * (i % 2) + 256)
            given[n, at, :] = made[i][:, :128]
            given[n + 1, at, :] = made[i][:, 128:]
        give(k).start()
        if k == 0:
            come.wait()
            go.start()
    for k in range(STEPS):
        give(k).wait()
    go.wait()


def local(initial_state, cotangent, gate_bank, slice_index, mode_order):
    hbm = pl.BlockSpec(memory_space=pl.ANY)
    vm = pl.BlockSpec(memory_space=pltpu.VMEM)
    sm = pl.BlockSpec(memory_space=pltpu.SMEM)
    big = lambda *shape: pltpu.VMEM(shape, BF)
    wide = lambda *shape: pltpu.VMEM(shape, F32)
    sem = lambda *shape: pltpu.SemaphoreType.DMA(shape)
    backs, sums = pl.pallas_call(
        kernel,
        out_shape=(jax.ShapeDtypeStruct((2, 16, 128, 256), BF), jax.ShapeDtypeStruct((3, 2, 128, 128), F32)),
        in_specs=[hbm, hbm, hbm, sm, sm],
        out_specs=(hbm, vm),
        scratch_shapes=[
            big(16, 4, 128, 128), big(16, 4, 128, 128), big(3, 4, 2, 128, 128), wide(3, 128, 128),
            big(256, 256), big(256, 256), big(256, 256), big(256, 256), big(64, 256), big(256, 256), big(256, 256),
            big(64, 4, 16, 256), big(64, 4, 16, 256), big(8, 128, 16, 256), big(2, 128, 16, 256),
            big(128, 32, 256), big(32, 128, 256), big(32, 128, 256), big(32, 128, 256),
            big(32, 128, 256), big(32, 128, 256), big(32, 128, 256),
            wide(4, 128, 128), wide(4, 128, 128), wide(9, 192, 128), wide(8, 24, 128), wide(4, 192, 128),
            sem(3), sem(64), sem(64), sem(64), sem(64), sem(2), sem(2, 8), sem(2, 8), sem(2, 8), sem(2, 8), sem(2, PIECES), sem(2, PIECES),
            sem(4), sem(4), sem(8), sem(8), sem(8), sem(8), sem(8), sem(8), sem(4), sem(4),
        ],
        compiler_params=pltpu.CompilerParams(collective_id=0, has_side_effects=True, vmem_limit_bytes=54 << 20),
        name="gradients",
    )(
        cotangent.reshape(16, 4, 128, 128), initial_state.reshape(16, 4, 128, 128),
        gate_bank, slice_index, mode_order,
    )
    out, grads = pl.pallas_call(
        finish,
        out_shape=(jax.ShapeDtypeStruct((16, 512, 128), BF), jax.ShapeDtypeStruct((3, 2, 128, 128), F32)),
        in_specs=[hbm, hbm],
        out_specs=(hbm, hbm),
        scratch_shapes=[big(256, 256), big(2, 16, 128, 256), big(16, 512, 128), wide(3, 2, 128, 128), sem(STEPS + 1), sem(STEPS + 1)],
        compiler_params=pltpu.CompilerParams(vmem_limit_bytes=60 << 20),
        name="outputs",
    )(backs, sums)
    return grads, out.reshape(16, 128, 2, 2, 128)


def solution(mesh):
    in_specs = (P("grp", "mem", None, None, None), P("grp", "mem", None, None, None), P(), P(), P())
    out_specs = (P(), P("grp", None, "mem", None, None))
    return jax.shard_map(local, mesh=mesh, in_specs=in_specs, out_specs=out_specs, check_vma=False)
```

```python
import jax
import jax.numpy as jnp
from jax import lax
from jax.experimental import pallas as pl
from jax.experimental.pallas import tpu as pltpu
from jax.sharding import PartitionSpec as P

MESH = pl.DeviceIdType.MESH
BF = jnp.bfloat16
F32 = jnp.float32
HIGH = lax.Precision.HIGHEST
NX, NY, NZ, NC = 4, 4, 8, 2
Z_ORDER = (4, 3, 5, 2, 6, 1, 7)
LAG = 3
PIECES = 8
EARLY = 2
PUMP = (2, 0, 1, 0, 2, 0, 1, 0)
X_FIRST = 8
STEPS = 2


def grid(shape):
    return lax.broadcasted_iota(jnp.int32, shape, 0), lax.broadcasted_iota(jnp.int32, shape, 1)


def block_turn():
    row, col = grid((256, 256))
    return ((row & 15) * 16 + (row >> 4) == col).astype(F32).astype(BF)


def output_turn():
    row, col = grid((256, 256))
    m = row >> 2
    stored = (m & 35) + ((m >> 2) & 1) * 16 + ((m >> 3) & 3) * 4
    return ((row & 3) * 64 + stored == col).astype(F32).astype(BF)


def index_table(order, number, stored):
    row, col = grid((128, 128))
    if stored:
        row = (row & 99) + ((row >> 4) & 1) * 4 + ((row >> 2) & 3) * 8
    mapped = jnp.zeros((128, 128), jnp.int32)
    for b in range(7):
        mapped = mapped + (((row >> b) & 1) << order[number, b])
    return (mapped == col).astype(F32)


def dot(a, b):
    return jnp.dot(a, b, preferred_element_type=F32)


def dot_nt(a, b):
    return lax.dot_general(a, b, (((1,), (1,)), ((), ())), preferred_element_type=F32)


def dot_tn(a, b):
    return lax.dot_general(a, b, (((0,), (0,)), ((), ())), preferred_element_type=F32)


def planes_down(a, b):
    top = jnp.concatenate([a[:, :128], b[:, :128]], axis=1)
    low = jnp.concatenate([a[:, 128:], b[:, 128:]], axis=1)
    return jnp.concatenate([top, low], axis=0)


def planes_up(o, which):
    half = o.shape[0] // 2
    lanes = slice(128 * which, 128 * which + 128)
    return jnp.concatenate([o[:half, lanes], o[half:, lanes]], axis=1)


def with_turned(l):
    return jnp.concatenate([l, jnp.concatenate([-l[:, 128:], l[:, :128]], axis=1)], axis=0)


def batches(count, size, load, compute, store):
    def body(i, carry):
        made = [compute(v) for v in [load(i * size + u) for u in range(size)]]
        for u in range(size):
            store(i * size + u, made[u])
        return carry

    lax.fori_loop(0, count // size, body, 0)


def kernel(
    c_in, x_in, bank_in, slices, order,
    sgr, eout,
    craw, xraw, bank, pickers,
    w1f, w1b, w2f, w2b, w3b, w3all, turn,
    csend, xsend, cmid, xmid, call, xq, b2, b2t, b1t, sg, xt, l1t, l2t, e, rx, ryc, rz, fin,
    in_s, cy_ss, cy_rs, xy_ss, xy_rs, c_ss, c_rs, x_ss, x_rs, c_own, x_own, g_ss, g_rs, f_ss, f_rs, s_ss, s_rs,
    e1s, e1r, e2s, e2r, e3s, e3r, e4s, e4r, e5s, e5r,
):
    grp, mem = lax.axis_index("grp"), lax.axis_index("mem")
    x, zh = grp // 2, grp % 2
    y, zl, c = mem // 8, (mem // 2) % 4, mem % 2
    z = zh * 4 + zl

    def device(dx, dy, dz, dc):
        x2, y2, z2, c2 = (x + dx) % NX, (y + dy) % NY, (z + dz) % NZ, (c + dc) % NC
        return (x2 * 2 + z2 // 4, (y2 * 4 + z2 % 4) * 2 + c2)

    def group(q):
        p = q // 2
        return 2 * (p + (p // 2) * (1 - 2 * (p % 2))) + q % 2

    loads = [pltpu.make_async_copy(a, b, in_s.at[i]) for i, (a, b) in enumerate(((c_in, craw), (x_in, xraw), (bank_in, bank)))]
    for load in loads:
        load.start()
    bar = pltpu.get_barrier_semaphore()

    for g in range(1, 8):
        pl.semaphore_signal(bar, inc=1, device_id=device(0, g // 2, 0, g % 2), device_id_type=MESH)
    for dz in range(1, NZ):
        pl.semaphore_signal(bar, inc=1, device_id=device(0, 0, dz, 0), device_id_type=MESH)
    for dx in range(1, NX):
        pl.semaphore_signal(bar, inc=1, device_id=device(dx, 0, 0, 0), device_id_type=MESH)

    def extract(raw, send, dy):
        first = 2 * ((y + dy) % NY)
        loaded = []
        for i in range(4):
            mp, rows = i // 2, pl.ds(pl.multiple_of(16 * (first + i % 2), 16), 16)
            loaded.append(jnp.concatenate([raw[:, 2 * mp + mm, rows, :].reshape(256, 128) for mm in range(2)], axis=1))
        made = [dot(turn[...], v).astype(BF) for v in loaded]
        for i in range(4):
            mp = i // 2
            for mm in range(2):
                for r in range(8):
                    w = 8 * (i % 2) + r
                    for cc in range(2):
                        q = (r * 2 + cc) * 16
                        send[(y + dy) % NY, w // 2 % 2, w // 4 + 4 * (w % 2), 2 * mp + mm, :, cc * 128:cc * 128 + 128] = made[i][q:q + 16, mm * 128:mm * 128 + 128]

    turn[...] = block_turn()
    loads[0].wait()
    extract(craw, csend, 0)
    pl.semaphore_wait(bar, 17)

    def make_gates():
        for s in range(3):
            pickers[s] = index_table(order, s, s == 1)
            small = pickers[s].astype(BF)
            planes, turned = [], []
            for q in range(2):
                chosen = bank[s, slices[s], q]
                planes.append(dot_nt(dot(small, chosen).astype(BF), small).astype(BF))
                turned.append(dot_nt(dot_nt(small, chosen).astype(BF), small).astype(BF))
            whole, flipped = ((w1b, w1f), (w2f, w2b), (None, w3all))[s]
            if whole is not None:
                whole[0:128, 0:128] = planes[0]
                whole[0:128, 128:256] = -planes[1]
                whole[128:256, 0:128] = planes[1]
                whole[128:256, 128:256] = planes[0]
            flipped[0:128, 0:128] = turned[0]
            flipped[0:128, 128:256] = turned[1]
            flipped[128:256, 0:128] = -turned[1]
            flipped[128:256, 128:256] = turned[0]
        at = pl.multiple_of(32 * x, 32)
        w3b[0:32, :] = w3all[pl.ds(at, 32), :]
        w3b[32:64, :] = w3all[pl.ds(128 + at, 32), :]

    def m_of(g):
        dy, dc = g // 2, g % 2
        return pl.multiple_of(((y + NY - dy) % NY) * 32 + ((c + NC - dc) % NC) * 16, 16)

    def place(dz):
        return (z + dz + 6) % NZ

    def mover(send, mid, land, spot, y_ss, y_rs, z_ss, z_rs, own_s):
        def over_y(g):
            dy, dc = g // 2, g % 2
            return pltpu.make_async_remote_copy(
                src_ref=send.at[(y + dy) % NY, (c + dc) % NC], dst_ref=mid.at[g],
                send_sem=y_ss.at[g], recv_sem=y_rs.at[g], device_id=device(0, dy, 0, dc), device_id_type=MESH)

        def source(g, dz, own):
            return send.at[y, c, place(dz)] if own else mid.at[g, place(dz)]

        def target(g):
            return land.at[spot, pl.ds(pl.multiple_of(m_of(g) + 4 * zl, 4), 4)]

        def over_z(g, dz, own=False):
            return pltpu.make_async_remote_copy(
                src_ref=source(g, dz, own), dst_ref=target(g), send_sem=z_ss.at[g, dz], recv_sem=z_rs.at[g, dz],
                device_id=device(0, 0, dz, 0), device_id_type=MESH)

        def stay(g, own=False):
            return pltpu.make_async_copy(source(g, 0, own), target(g), own_s.at[g])

        def go(g, own=False):
            for dz in Z_ORDER:
                over_z(g, dz, own).start()
            stay(g, own).start()

        def pass_on(g):
            over_y(g).wait_recv()
            go(g)

        def come(g):
            for dz in Z_ORDER:
                over_z(g, dz).wait_recv()
            stay(g).wait()

        def gone():
            def body(g, carry):
                @pl.when(g > 0)
                def _():
                    over_y(g).wait_send()

                for dz in Z_ORDER:
                    over_z(g, dz).wait_send()
                return carry

            lax.fori_loop(0, 8, body, 0)

        return over_y, go, pass_on, come, gone

    c_over_y, c_go, c_pass_on, c_come, c_gone = mover(csend, cmid, call, grp, cy_ss, cy_rs, c_ss, c_rs, c_own)
    x_over_y, x_go, x_pass_on, x_come, x_gone = mover(xsend, xmid, xq, zh, xy_ss, xy_rs, x_ss, x_rs, x_own)

    c_go(0, True)
    c_over_y(1).start()

    def c_start(p, carry):
        g = group(2 * p)
        extract(craw, csend, g // 2)
        c_over_y(g).start()
        c_over_y(g + 1).start()
        return carry

    lax.fori_loop(1, 4, c_start, 0)
    c_pass_on(1)
    loads[1].wait()

    def x_start(p, carry):
        g = group(2 * p)
        extract(xraw, xsend, g // 2)

        @pl.when(p > 0)
        def _():
            x_over_y(g).start()

        x_over_y(g + 1).start()
        return carry

    lax.fori_loop(0, 4, x_start, 0)

    def near(g, way):
        part = call.at[pl.ds(2 * x, 2), pl.ds(m_of(g), 16)]
        return pltpu.make_async_remote_copy(
            src_ref=part, dst_ref=part, send_sem=g_ss.at[way, g], recv_sem=g_rs.at[way, g],
            device_id=device(1 if way == 0 else NX - 1, 0, 0, 0), device_id_type=MESH)

    def far(g, way):
        owner = (x + NX - 1) % NX if way == 0 else (x + 1) % NX
        part = call.at[pl.ds(2 * owner, 2), pl.ds(m_of(g) + 8 * way, 8)]
        return pltpu.make_async_remote_copy(
            src_ref=part, dst_ref=part, send_sem=f_ss.at[way, g], recv_sem=f_rs.at[way, g],
            device_id=device(1 if way == 0 else NX - 1, 0, 0, 0), device_id_type=MESH)

    def relay(g):
        for way in range(2):
            near(g, way).wait_recv()
            far(g, way).start()

    def arrive(h):
        g = group(h)
        c_come(g)
        near(g, 0).start()
        near(g, 1).start()

    def early(q, carry):
        c_pass_on(group(q))

        @pl.when(q >= LAG)
        def _():
            arrive(q - LAG)

        @pl.when(q > LAG)
        def _():
            relay(group(q - LAG - 1))

        return carry

    lax.fori_loop(2, 8, early, 0)
    loads[2].wait()
    make_gates()
    x_go(0, True)
    x_pass_on(1)

    def late(h, carry):
        arrive(h)
        relay(group(h - 1))
        x_pass_on(group(2 * (h + LAG - 7)))
        x_pass_on(group(2 * (h + LAG - 7) + 1))
        return carry

    lax.fori_loop(8 - LAG, 8, late, 0)
    relay(group(7))

    def all_n(m):
        return call[:, m].reshape(128, 256)

    def third(h, carry):
        g = group(h)
        far(g, 0).wait_recv()
        far(g, 1).wait_recv()

        base = m_of(g)
        made = [planes_down(all_n(base + 2 * p), all_n(base + 2 * p + 1)) for p in range(8)]
        made = [dot(w3b[...], v).astype(BF) for v in made]
        for p in range(8):
            b2[base + 2 * p] = planes_up(made[p], 0)
            b2[base + 2 * p + 1] = planes_up(made[p], 1)
        return carry

    lax.fori_loop(0, 8, third, 0)

    def turn_all(src, dst, to_rows):
        def places(i):
            return pl.ds(pl.multiple_of(16 * (i % 8), 16), 16), pl.ds(pl.multiple_of(16 * (i // 8), 16), 16)

        def load(i):
            m, n = places(i)
            if len(src.shape) == 4:
                return src[i // 8, m].reshape(256, 256)
            return (src[m, n, :] if to_rows else src[n, m, :]).reshape(256, 256)

        def store(i, o):
            m, n = places(i)
            if to_rows:
                dst[n, m, :] = o.reshape(16, 16, 256)
            else:
                dst[m, n, :] = o.reshape(16, 16, 256)

        batches(16, 8, load, lambda v: dot(turn[...], v).astype(BF), store)

    def gate_two(src, dst, w, base, pairs):
        def store(i, o):
            dst[base + 2 * i] = planes_up(o, 0)
            dst[base + 2 * i + 1] = planes_up(o, 1)

        batches(pairs, 4, lambda i: planes_down(src[base + 2 * i], src[base + 2 * i + 1]),
                lambda v: dot(w[...], v).astype(BF), store)

    def gate_one(src, dst, w, base, pairs):
        def store(i, o):
            dst[pl.ds(base + 2 * i, 2)] = o.reshape(2, 128, 256)

        batches(pairs, 4, lambda i: src[pl.ds(base + 2 * i, 2)].reshape(256, 256),
                lambda v: dot(v, w[...]).astype(BF), store)

    s_here = (z + 6) % NZ
    part_here = s_here // 4

    per = 16 // PIECES

    def back(half, k):
        z_to = 4 * half + s_here % 4
        return pltpu.make_async_remote_copy(
            src_ref=sg.at[pl.ds(16 * half + per * k, per)], dst_ref=sgr.at[part_here, pl.ds(per * k, per)],
            send_sem=s_ss.at[half, k], recv_sem=s_rs.at[part_here, k],
            device_id=device(0, 0, z_to + NZ - z, 0), device_id_type=MESH)

    turn_all(b2, b2t, True)
    for k in range(2):
        for half in range(2):
            n = 16 * half + 8 * k
            gate_two(b2t, b1t, w2b, n, 4)
            gate_one(b1t, sg, w1b, n, 4)

    def pump(stop):
        first = EARLY + sum(PUMP[:stop])
        for j in range(first, PIECES if stop == len(PUMP) - 1 else first + PUMP[stop]):
            back(0, j).start()
            back(1, j).start()

    def x_arrive(h, carry):
        x_come(group(h))
        return carry

    lax.fori_loop(0, X_FIRST, x_arrive, 0)
    for j in range(EARLY):
        back(0, j).start()
        back(1, j).start()
    lax.fori_loop(X_FIRST, 8, x_arrive, 0)
    turn_all(xq, xt, True)
    gate_one(xt, l1t, w1f, 0, 16)

    def grad_two(i, acc):
        for u in range(8):
            acc = acc + dot_nt(b2t[8 * i + u], with_turned(l1t[8 * i + u]))
        return acc

    acc = lax.fori_loop(0, 4, grad_two, jnp.zeros((128, 256), F32))
    for k in range(NX):
        e[k, 64:128, :] = acc[64 * (k % 2):64 * (k % 2) + 64, 128 * (k // 2):128 * (k // 2) + 128]

    def grad_one(i, acc):
        rows = pl.ds(8 * i, 8)
        return acc + dot_tn(b1t[rows].reshape(1024, 256), xt[rows].reshape(1024, 256))

    acc = lax.fori_loop(0, 4, grad_one, jnp.zeros((256, 256), F32))
    for k in range(2):
        i = slice(64 * k, 64 * k + 64)
        j = slice(128 + 64 * k, 128 + 64 * k + 64)
        e[k, 0:64, :] = acc[i, 0:128] + acc[j, 128:256]
        e[2 + k, 0:64, :] = acc[j, 0:128] - acc[i, 128:256]

    def one(dx):
        to = (x + dx) % NX
        return pltpu.make_async_remote_copy(
            src_ref=e.at[to], dst_ref=rx.at[x],
            send_sem=e1s.at[dx], recv_sem=e1r.at[dx], device_id=device(dx, 0, 0, 0), device_id_type=MESH)

    for dx in range(1, NX):
        one(dx).start()
    rx[x] = e[x]

    pump(0)
    gate_two(l1t, l2t, w2f, 0, 16)
    turn_all(l2t, b2, False)

    def grad_three(i, acc):
        for p in range(16):
            acc = acc + dot_nt(all_n(16 * i + p), with_turned(b2[16 * i + p]))
        return acc

    acc = lax.fori_loop(0, 8, grad_three, jnp.zeros((128, 64), F32))
    ryc[8, 128:192, :] = jnp.transpose(jnp.concatenate([acc, jnp.zeros((128, 64), F32)], axis=1))[0:64, :]

    def yc(k):
        return ((y + k // 2) % NY) * 2 + (c + k % 2) % NC

    def two(k):
        to = yc(k)
        return pltpu.make_async_remote_copy(
            src_ref=ryc.at[8, pl.ds(pl.multiple_of(24 * to, 8), 24), :],
            dst_ref=ryc.at[y * 2 + c, pl.ds(0, 24), :],
            send_sem=e2s.at[k], recv_sem=e2r.at[k], device_id=device(0, k // 2, 0, k % 2), device_id_type=MESH)

    def three(dz):
        return pltpu.make_async_remote_copy(
            src_ref=rz.at[z], dst_ref=rz.at[z],
            send_sem=e3s.at[dz], recv_sem=e3r.at[dz], device_id=device(0, 0, dz, 0), device_id_type=MESH)

    def four(k):
        rows = fin.at[x, pl.ds(pl.multiple_of(24 * (y * 2 + c), 8), 24), :]
        return pltpu.make_async_remote_copy(
            src_ref=rows, dst_ref=rows,
            send_sem=e4s.at[k], recv_sem=e4r.at[k], device_id=device(0, k // 2, 0, k % 2), device_id_type=MESH)

    def five(dx):
        rows = fin.at[x]
        return pltpu.make_async_remote_copy(
            src_ref=rows, dst_ref=rows,
            send_sem=e5s.at[dx], recv_sem=e5r.at[dx], device_id=device(dx, 0, 0, 0), device_id_type=MESH)

    pump(1)
    for dx in range(1, NX):
        one(dx).wait_recv()
    ryc[8, 0:128, :] = (rx[0] + rx[1]) + (rx[2] + rx[3])
    for k in range(1, 8):
        two(k).start()
    ryc[y * 2 + c, 0:24, :] = ryc[8, pl.ds(pl.multiple_of(24 * (y * 2 + c), 8), 24), :]
    pump(2)
    for k in range(1, 8):
        two(k).wait_recv()
    pump(3)
    total = ryc[0, 0:24, :]
    for k in range(1, 8):
        total = total + ryc[k, 0:24, :]
    rz[z] = total
    for dz in range(1, NZ):
        three(dz).start()
    pump(4)
    for dz in range(1, NZ):
        three(dz).wait_recv()
    pump(5)
    total = rz[0]
    for k in range(1, NZ):
        total = total + rz[k]
    fin[x, pl.ds(pl.multiple_of(24 * (y * 2 + c), 8), 24), :] = total
    for k in range(1, 8):
        four(k).start()
    pump(6)
    for k in range(1, 8):
        four(k).wait_recv()
    for dx in range(1, NX):
        five(dx).start()
    pump(7)
    for dx in range(1, NX):
        five(dx).wait_recv()

    def exact(a, b, dims):
        return lax.dot_general(a, b, (dims, ((), ())), precision=HIGH, preferred_element_type=F32)

    factor = 1.0 / (128 * 64**0.5)
    sides = [(s, q) for s in range(3) for q in range(2)]

    def sums(s, q):
        if s < 2:
            return jnp.concatenate([fin[2 * q + k, 64 * s:64 * s + 64, :] for k in range(2)], axis=0)
        return jnp.concatenate([fin[k, 128 + 32 * q:160 + 32 * q, :] for k in range(NX)], axis=0)

    moved = [exact(pickers[s], sums(s, q), ((0,), (1,) if s == 2 else (0,))) for s, q in sides]
    for (s, q), part in zip(sides, moved):
        eout[s, q] = exact(part, pickers[s], ((1,), (0,))) * factor

    c_gone()
    x_gone()

    def g_gone(g, carry):
        for way in range(2):
            near(g, way).wait_send()
            far(g, way).wait_send()
        return carry

    lax.fori_loop(0, 8, g_gone, 0)
    for dx in range(1, NX):
        one(dx).wait_send()
        five(dx).wait_send()
    for k in range(1, 8):
        two(k).wait_send()
        three(k).wait_send()
        four(k).wait_send()

    def landed(part, k):
        return pltpu.make_async_remote_copy(
            src_ref=sg.at[pl.ds(0, per)], dst_ref=sgr.at[part, pl.ds(per * k, per)],
            send_sem=s_ss.at[0, k], recv_sem=s_rs.at[part, k],
            device_id=device(0, 0, 2, 0), device_id_type=MESH)

    for k in range(PIECES):
        for half in range(2):
            landed(half, k).wait_recv()
            back(half, k).wait_send()


def finish(back, sums, out, eout, outturn, sgr, given, held, in_s, out_s):
    per = 16 // STEPS
    come = pltpu.make_async_copy(sums, held, in_s.at[STEPS])
    go = pltpu.make_async_copy(held, eout, out_s.at[STEPS])

    def load(k):
        at = pl.ds(per * k, per)
        return pltpu.make_async_copy(back.at[:, at], sgr.at[:, at], in_s.at[k])

    def give(k):
        at = pl.ds(per * k, per)
        return pltpu.make_async_copy(given.at[at], out.at[at], out_s.at[k])

    for k in range(STEPS):
        load(k).start()
    come.start()
    outturn[...] = output_turn()
    for k in range(STEPS):
        load(k).wait()
        made = []
        for i in range(per):
            n, rows = per * k + 2 * (i // 2), slice(64 * (i % 2), 64 * (i % 2) + 64)
            sides = [jnp.concatenate([sgr[r, n + nn, rows, cc * 128:cc * 128 + 128] for r in range(2) for cc in range(2)], axis=0)
                     for nn in range(2)]
            made.append(dot(outturn[...], jnp.concatenate(sides, axis=1)).astype(BF))
        for i in range(per):
            n, at = per * k + 2 * (i // 2), slice(256 * (i % 2), 256 * (i % 2) + 256)
            given[n, at, :] = made[i][:, :128]
            given[n + 1, at, :] = made[i][:, 128:]
        give(k).start()
        if k == 0:
            come.wait()
            go.start()
    for k in range(STEPS):
        give(k).wait()
    go.wait()


def local(initial_state, cotangent, gate_bank, slice_index, mode_order):
    hbm = pl.BlockSpec(memory_space=pl.ANY)
    vm = pl.BlockSpec(memory_space=pltpu.VMEM)
    sm = pl.BlockSpec(memory_space=pltpu.SMEM)
    big = lambda *shape: pltpu.VMEM(shape, BF)
    wide = lambda *shape: pltpu.VMEM(shape, F32)
    sem = lambda *shape: pltpu.SemaphoreType.DMA(shape)
    backs, sums = pl.pallas_call(
        kernel,
        out_shape=(jax.ShapeDtypeStruct((2, 16, 128, 256), BF), jax.ShapeDtypeStruct((3, 2, 128, 128), F32)),
        in_specs=[hbm, hbm, hbm, sm, sm],
        out_specs=(hbm, vm),
        scratch_shapes=[
            big(16, 4, 128, 128), big(16, 4, 128, 128), big(3, 4, 2, 128, 128), wide(3, 128, 128),
            big(256, 256), big(256, 256), big(256, 256), big(256, 256), big(64, 256), big(256, 256), big(256, 256),
            big(4, 2, 8, 4, 16, 256), big(4, 2, 8, 4, 16, 256), big(8, 8, 4, 16, 256), big(8, 8, 4, 16, 256), big(8, 128, 16, 256), big(2, 128, 16, 256),
            big(128, 32, 256), big(32, 128, 256), big(32, 128, 256), big(32, 128, 256),
            big(32, 128, 256), big(32, 128, 256), big(32, 128, 256),
            wide(4, 128, 128), wide(4, 128, 128), wide(9, 192, 128), wide(8, 24, 128), wide(4, 192, 128),
            sem(3), sem(8), sem(8), sem(8), sem(8), sem(8, 8), sem(8, 8), sem(8, 8), sem(8, 8), sem(8), sem(8), sem(2, 8), sem(2, 8), sem(2, 8), sem(2, 8), sem(2, PIECES), sem(2, PIECES),
            sem(4), sem(4), sem(8), sem(8), sem(8), sem(8), sem(8), sem(8), sem(4), sem(4),
        ],
        compiler_params=pltpu.CompilerParams(collective_id=0, has_side_effects=True, vmem_limit_bytes=54 << 20),
        name="gradients",
    )(
        cotangent.reshape(16, 4, 128, 128), initial_state.reshape(16, 4, 128, 128),
        gate_bank, slice_index, mode_order,
    )
    out, grads = pl.pallas_call(
        finish,
        out_shape=(jax.ShapeDtypeStruct((16, 512, 128), BF), jax.ShapeDtypeStruct((3, 2, 128, 128), F32)),
        in_specs=[hbm, hbm],
        out_specs=(hbm, hbm),
        scratch_shapes=[big(256, 256), big(2, 16, 128, 256), big(16, 512, 128), wide(3, 2, 128, 128), sem(STEPS + 1), sem(STEPS + 1)],
        compiler_params=pltpu.CompilerParams(vmem_limit_bytes=60 << 20),
        name="outputs",
    )(backs, sums)
    return grads, out.reshape(16, 128, 2, 2, 128)


def solution(mesh):
    in_specs = (P("grp", "mem", None, None, None), P("grp", "mem", None, None, None), P(), P(), P())
    out_specs = (P(), P("grp", None, "mem", None, None))
    return jax.shard_map(local, mesh=mesh, in_specs=in_specs, out_specs=out_specs, check_vma=False)
```

```python
import jax
import jax.numpy as jnp
from jax import lax
from jax.experimental import pallas as pl
from jax.experimental.pallas import tpu as pltpu
from jax.sharding import PartitionSpec as P

MESH = pl.DeviceIdType.MESH
BF = jnp.bfloat16
F32 = jnp.float32
HIGH = lax.Precision.HIGHEST
NX, NY, NZ, NC = 4, 4, 8, 2
Z_ORDER = (4, 3, 5, 2, 6, 1, 7)
LAG = 3
PIECES = 8
EARLY = 1
PUMP = (2, 0, 1, 0, 2, 0, 1, 1)
X_FIRST = 6
STEPS = 2


def grid(shape):
    return lax.broadcasted_iota(jnp.int32, shape, 0), lax.broadcasted_iota(jnp.int32, shape, 1)


def block_turn():
    row, col = grid((256, 256))
    return ((row & 15) * 16 + (row >> 4) == col).astype(F32).astype(BF)


def output_turn():
    row, col = grid((256, 256))
    m = row >> 2
    stored = (m & 35) + ((m >> 2) & 1) * 16 + ((m >> 3) & 3) * 4
    return ((row & 3) * 64 + stored == col).astype(F32).astype(BF)


def index_table(order, number, stored):
    row, col = grid((128, 128))
    if stored:
        row = (row & 99) + ((row >> 4) & 1) * 4 + ((row >> 2) & 3) * 8
    mapped = jnp.zeros((128, 128), jnp.int32)
    for b in range(7):
        mapped = mapped + (((row >> b) & 1) << order[number, b])
    return (mapped == col).astype(F32)


def dot(a, b):
    return jnp.dot(a, b, preferred_element_type=F32)


def dot_nt(a, b):
    return lax.dot_general(a, b, (((1,), (1,)), ((), ())), preferred_element_type=F32)


def dot_tn(a, b):
    return lax.dot_general(a, b, (((0,), (0,)), ((), ())), preferred_element_type=F32)


def planes_down(a, b):
    top = jnp.concatenate([a[:, :128], b[:, :128]], axis=1)
    low = jnp.concatenate([a[:, 128:], b[:, 128:]], axis=1)
    return jnp.concatenate([top, low], axis=0)


def planes_up(o, which):
    half = o.shape[0] // 2
    lanes = slice(128 * which, 128 * which + 128)
    return jnp.concatenate([o[:half, lanes], o[half:, lanes]], axis=1)


def with_turned(l):
    return jnp.concatenate([l, jnp.concatenate([-l[:, 128:], l[:, :128]], axis=1)], axis=0)


def batches(count, size, load, compute, store):
    def body(i, carry):
        made = [compute(v) for v in [load(i * size + u) for u in range(size)]]
        for u in range(size):
            store(i * size + u, made[u])
        return carry

    lax.fori_loop(0, count // size, body, 0)


def kernel(
    c_in, x_in, bank_in, slices, order,
    sgr, eout,
    craw, xraw, bank, pickers,
    w1f, w1b, w2f, w2b, w3b, w3all, turn,
    csend, xsend, cmid, xmid, call, xq, b2, b2t, b1t, sg, l1t, l2t, e, rx, ryc, rz, fin,
    in_s, cy_ss, cy_rs, xy_ss, xy_rs, c_ss, c_rs, x_ss, x_rs, c_own, x_own, g_ss, g_rs, f_ss, f_rs, s_ss, s_rs,
    e1s, e1r, e2s, e2r, e3s, e3r, e4s, e4r, e5s, e5r,
):
    grp, mem = lax.axis_index("grp"), lax.axis_index("mem")
    x, zh = grp // 2, grp % 2
    y, zl, c = mem // 8, (mem // 2) % 4, mem % 2
    z = zh * 4 + zl

    def device(dx, dy, dz, dc):
        x2, y2, z2, c2 = (x + dx) % NX, (y + dy) % NY, (z + dz) % NZ, (c + dc) % NC
        return (x2 * 2 + z2 // 4, (y2 * 4 + z2 % 4) * 2 + c2)

    def group(q):
        p = q // 2
        return 2 * (p + (p // 2) * (1 - 2 * (p % 2))) + q % 2

    loads = [pltpu.make_async_copy(a, b, in_s.at[i]) for i, (a, b) in enumerate(((c_in, craw), (x_in, xraw), (bank_in, bank)))]
    for load in loads:
        load.start()
    bar = pltpu.get_barrier_semaphore()

    for g in range(1, 8):
        pl.semaphore_signal(bar, inc=1, device_id=device(0, g // 2, 0, g % 2), device_id_type=MESH)
    for dz in range(1, NZ):
        pl.semaphore_signal(bar, inc=1, device_id=device(0, 0, dz, 0), device_id_type=MESH)
    for dx in range(1, NX):
        pl.semaphore_signal(bar, inc=1, device_id=device(dx, 0, 0, 0), device_id_type=MESH)

    def extract(raw, send, dy):
        first = 2 * ((y + dy) % NY)
        loaded = []
        for i in range(4):
            mp, rows = i // 2, pl.ds(pl.multiple_of(16 * (first + i % 2), 16), 16)
            loaded.append(jnp.concatenate([raw[:, 2 * mp + mm, rows, :].reshape(256, 128) for mm in range(2)], axis=1))
        made = [dot(turn[...], v).astype(BF) for v in loaded]
        for i in range(4):
            mp = i // 2
            for mm in range(2):
                for r in range(8):
                    w = 8 * (i % 2) + r
                    for cc in range(2):
                        q = (r * 2 + cc) * 16
                        send[(y + dy) % NY, w // 2 % 2, w // 4 + 4 * (w % 2), 2 * mp + mm, :, cc * 128:cc * 128 + 128] = made[i][q:q + 16, mm * 128:mm * 128 + 128]

    turn[...] = block_turn()
    loads[0].wait()
    extract(craw, csend, 0)
    pl.semaphore_wait(bar, 17)

    def make_gates():
        for s in range(3):
            pickers[s] = index_table(order, s, s == 1)
            small = pickers[s].astype(BF)
            planes, turned = [], []
            for q in range(2):
                chosen = bank[s, slices[s], q]
                planes.append(dot_nt(dot(small, chosen).astype(BF), small).astype(BF))
                turned.append(dot_nt(dot_nt(small, chosen).astype(BF), small).astype(BF))
            whole, flipped = ((w1b, w1f), (w2f, w2b), (None, w3all))[s]
            if whole is not None:
                whole[0:128, 0:128] = planes[0]
                whole[0:128, 128:256] = -planes[1]
                whole[128:256, 0:128] = planes[1]
                whole[128:256, 128:256] = planes[0]
            flipped[0:128, 0:128] = turned[0]
            flipped[0:128, 128:256] = turned[1]
            flipped[128:256, 0:128] = -turned[1]
            flipped[128:256, 128:256] = turned[0]
        at = pl.multiple_of(32 * x, 32)
        w3b[0:32, :] = w3all[pl.ds(at, 32), :]
        w3b[32:64, :] = w3all[pl.ds(128 + at, 32), :]

    def m_of(g):
        dy, dc = g // 2, g % 2
        return pl.multiple_of(((y + NY - dy) % NY) * 32 + ((c + NC - dc) % NC) * 16, 16)

    def place(dz):
        return (z + dz + 6) % NZ

    def mover(send, mid, land, spot, y_ss, y_rs, z_ss, z_rs, own_s):
        def over_y(g):
            dy, dc = g // 2, g % 2
            return pltpu.make_async_remote_copy(
                src_ref=send.at[(y + dy) % NY, (c + dc) % NC], dst_ref=mid.at[g],
                send_sem=y_ss.at[g], recv_sem=y_rs.at[g], device_id=device(0, dy, 0, dc), device_id_type=MESH)

        def source(g, dz, own):
            return send.at[y, c, place(dz)] if own else mid.at[g, place(dz)]

        def target(g):
            return land.at[spot, pl.ds(pl.multiple_of(m_of(g) + 4 * zl, 4), 4)]

        def over_z(g, dz, own=False):
            return pltpu.make_async_remote_copy(
                src_ref=source(g, dz, own), dst_ref=target(g), send_sem=z_ss.at[g, dz], recv_sem=z_rs.at[g, dz],
                device_id=device(0, 0, dz, 0), device_id_type=MESH)

        def stay(g, own=False):
            return pltpu.make_async_copy(source(g, 0, own), target(g), own_s.at[g])

        def go(g, own=False):
            for dz in Z_ORDER:
                over_z(g, dz, own).start()
            stay(g, own).start()

        def pass_on(g):
            over_y(g).wait_recv()
            go(g)

        def come(g):
            for dz in Z_ORDER:
                over_z(g, dz).wait_recv()
            stay(g).wait()

        def gone():
            def body(g, carry):
                @pl.when(g > 0)
                def _():
                    over_y(g).wait_send()

                for dz in Z_ORDER:
                    over_z(g, dz).wait_send()
                return carry

            lax.fori_loop(0, 8, body, 0)

        return over_y, go, pass_on, come, gone

    c_over_y, c_go, c_pass_on, c_come, c_gone = mover(csend, cmid, call, grp, cy_ss, cy_rs, c_ss, c_rs, c_own)
    x_over_y, x_go, x_pass_on, x_come, x_gone = mover(xsend, xmid, xq, zh, xy_ss, xy_rs, x_ss, x_rs, x_own)

    c_go(0, True)
    c_over_y(1).start()

    def c_start(p, carry):
        g = group(2 * p)
        extract(craw, csend, g // 2)
        c_over_y(g).start()
        c_over_y(g + 1).start()
        return carry

    lax.fori_loop(1, 4, c_start, 0)
    c_pass_on(1)
    loads[1].wait()

    def x_start(p, carry):
        g = group(2 * p)
        extract(xraw, xsend, g // 2)

        @pl.when(p > 0)
        def _():
            x_over_y(g).start()

        x_over_y(g + 1).start()
        return carry

    lax.fori_loop(0, 4, x_start, 0)

    def near(g, way):
        part = call.at[pl.ds(2 * x, 2), pl.ds(m_of(g), 16)]
        return pltpu.make_async_remote_copy(
            src_ref=part, dst_ref=part, send_sem=g_ss.at[way, g], recv_sem=g_rs.at[way, g],
            device_id=device(1 if way == 0 else NX - 1, 0, 0, 0), device_id_type=MESH)

    def far(g, way):
        owner = (x + NX - 1) % NX if way == 0 else (x + 1) % NX
        part = call.at[pl.ds(2 * owner, 2), pl.ds(m_of(g) + 8 * way, 8)]
        return pltpu.make_async_remote_copy(
            src_ref=part, dst_ref=part, send_sem=f_ss.at[way, g], recv_sem=f_rs.at[way, g],
            device_id=device(1 if way == 0 else NX - 1, 0, 0, 0), device_id_type=MESH)

    def relay(g):
        for way in range(2):
            near(g, way).wait_recv()
            far(g, way).start()

    def arrive(h):
        g = group(h)
        c_come(g)
        near(g, 0).start()
        near(g, 1).start()

    def early(q, carry):
        c_pass_on(group(q))

        @pl.when(q >= LAG)
        def _():
            arrive(q - LAG)

        @pl.when(q > LAG)
        def _():
            relay(group(q - LAG - 1))

        return carry

    lax.fori_loop(2, 8, early, 0)
    loads[2].wait()
    make_gates()
    x_go(0, True)
    x_pass_on(1)

    def late(h, carry):
        arrive(h)
        relay(group(h - 1))
        x_pass_on(group(2 * (h + LAG - 7)))
        x_pass_on(group(2 * (h + LAG - 7) + 1))
        return carry

    lax.fori_loop(8 - LAG, 8, late, 0)
    relay(group(7))

    def all_n(m):
        return call[:, m].reshape(128, 256)

    def third(h, carry):
        g = group(h)
        far(g, 0).wait_recv()
        far(g, 1).wait_recv()

        base = m_of(g)
        made = [planes_down(all_n(base + 2 * p), all_n(base + 2 * p + 1)) for p in range(8)]
        made = [dot(w3b[...], v).astype(BF) for v in made]
        for p in range(8):
            b2[base + 2 * p] = planes_up(made[p], 0)
            b2[base + 2 * p + 1] = planes_up(made[p], 1)
        return carry

    lax.fori_loop(0, 8, third, 0)

    def turn_all(src, dst, to_rows):
        def places(i):
            return pl.ds(pl.multiple_of(16 * (i % 8), 16), 16), pl.ds(pl.multiple_of(16 * (i // 8), 16), 16)

        def load(i):
            m, n = places(i)
            if len(src.shape) == 4:
                return src[i // 8, m].reshape(256, 256)
            return (src[m, n, :] if to_rows else src[n, m, :]).reshape(256, 256)

        def store(i, o):
            m, n = places(i)
            if to_rows:
                dst[n, m, :] = o.reshape(16, 16, 256)
            else:
                dst[m, n, :] = o.reshape(16, 16, 256)

        batches(16, 8, load, lambda v: dot(turn[...], v).astype(BF), store)

    def gate_two(src, dst, w, base, pairs):
        def store(i, o):
            dst[base + 2 * i] = planes_up(o, 0)
            dst[base + 2 * i + 1] = planes_up(o, 1)

        batches(pairs, 4, lambda i: planes_down(src[base + 2 * i], src[base + 2 * i + 1]),
                lambda v: dot(w[...], v).astype(BF), store)

    def gate_one(src, dst, w, base, pairs):
        def store(i, o):
            dst[pl.ds(base + 2 * i, 2)] = o.reshape(2, 128, 256)

        batches(pairs, 4, lambda i: src[pl.ds(base + 2 * i, 2)].reshape(256, 256),
                lambda v: dot(v, w[...]).astype(BF), store)

    s_here = (z + 6) % NZ
    part_here = s_here // 4

    per = 16 // PIECES

    def back(half, k):
        z_to = 4 * half + s_here % 4
        return pltpu.make_async_remote_copy(
            src_ref=sg.at[pl.ds(16 * half + per * k, per)], dst_ref=sgr.at[part_here, pl.ds(per * k, per)],
            send_sem=s_ss.at[half, k], recv_sem=s_rs.at[part_here, k],
            device_id=device(0, 0, z_to + NZ - z, 0), device_id_type=MESH)

    turn_all(b2, b2t, True)
    for k in range(2):
        for half in range(2):
            n = 16 * half + 8 * k
            gate_two(b2t, b1t, w2b, n, 4)
            gate_one(b1t, sg, w1b, n, 4)

    def pump(stop):
        first = EARLY + sum(PUMP[:stop])
        for j in range(first, PIECES if stop == len(PUMP) - 1 else first + PUMP[stop]):
            back(0, j).start()
            back(1, j).start()

    def x_arrive(h, acc):
        g = group(h)
        x_come(g)
        m = pl.ds(m_of(g), 16)
        rows = [dot(turn[...], xq[nb, m].reshape(256, 256)).astype(BF) for nb in range(2)]
        rows = jnp.concatenate(rows, axis=0)
        l1t[:, m, :] = dot(rows, w1f[...]).astype(BF).reshape(32, 16, 256)
        return acc + dot_tn(b1t[:, m, :].reshape(512, 256), rows)

    v1 = lax.fori_loop(0, X_FIRST, x_arrive, jnp.zeros((256, 256), F32))
    for j in range(EARLY):
        back(0, j).start()
        back(1, j).start()
    v1 = lax.fori_loop(X_FIRST, 8, x_arrive, v1)
    for k in range(2):
        i = slice(64 * k, 64 * k + 64)
        j = slice(128 + 64 * k, 128 + 64 * k + 64)
        e[k, 0:64, :] = v1[i, 0:128] + v1[j, 128:256]
        e[2 + k, 0:64, :] = v1[j, 0:128] - v1[i, 128:256]

    def grad_two(i, acc):
        for u in range(8):
            acc = acc + dot_nt(b2t[8 * i + u], with_turned(l1t[8 * i + u]))
        return acc

    acc = lax.fori_loop(0, 4, grad_two, jnp.zeros((128, 256), F32))
    for k in range(NX):
        e[k, 64:128, :] = acc[64 * (k % 2):64 * (k % 2) + 64, 128 * (k // 2):128 * (k // 2) + 128]

    def one(dx):
        to = (x + dx) % NX
        return pltpu.make_async_remote_copy(
            src_ref=e.at[to], dst_ref=rx.at[x],
            send_sem=e1s.at[dx], recv_sem=e1r.at[dx], device_id=device(dx, 0, 0, 0), device_id_type=MESH)

    for dx in range(1, NX):
        one(dx).start()
    rx[x] = e[x]

    pump(0)
    gate_two(l1t, l2t, w2f, 0, 16)
    turn_all(l2t, b2, False)

    def grad_three(i, acc):
        for p in range(32):
            acc = acc + dot_nt(all_n(32 * i + p), with_turned(b2[32 * i + p]))
        return acc

    acc = lax.fori_loop(0, 4, grad_three, jnp.zeros((128, 64), F32))
    ryc[8, 128:192, :] = jnp.transpose(jnp.concatenate([acc, jnp.zeros((128, 64), F32)], axis=1))[0:64, :]

    def yc(k):
        return ((y + k // 2) % NY) * 2 + (c + k % 2) % NC

    def two(k):
        to = yc(k)
        return pltpu.make_async_remote_copy(
            src_ref=ryc.at[8, pl.ds(pl.multiple_of(24 * to, 8), 24), :],
            dst_ref=ryc.at[y * 2 + c, pl.ds(0, 24), :],
            send_sem=e2s.at[k], recv_sem=e2r.at[k], device_id=device(0, k // 2, 0, k % 2), device_id_type=MESH)

    def three(dz):
        return pltpu.make_async_remote_copy(
            src_ref=rz.at[z], dst_ref=rz.at[z],
            send_sem=e3s.at[dz], recv_sem=e3r.at[dz], device_id=device(0, 0, dz, 0), device_id_type=MESH)

    def four(k):
        rows = fin.at[x, pl.ds(pl.multiple_of(24 * (y * 2 + c), 8), 24), :]
        return pltpu.make_async_remote_copy(
            src_ref=rows, dst_ref=rows,
            send_sem=e4s.at[k], recv_sem=e4r.at[k], device_id=device(0, k // 2, 0, k % 2), device_id_type=MESH)

    def five(dx):
        rows = fin.at[x]
        return pltpu.make_async_remote_copy(
            src_ref=rows, dst_ref=rows,
            send_sem=e5s.at[dx], recv_sem=e5r.at[dx], device_id=device(dx, 0, 0, 0), device_id_type=MESH)

    pump(1)
    for dx in range(1, NX):
        one(dx).wait_recv()
    ryc[8, 0:128, :] = (rx[0] + rx[1]) + (rx[2] + rx[3])
    for k in range(1, 8):
        two(k).start()
    ryc[y * 2 + c, 0:24, :] = ryc[8, pl.ds(pl.multiple_of(24 * (y * 2 + c), 8), 24), :]
    pump(2)
    for k in range(1, 8):
        two(k).wait_recv()
    pump(3)
    total = ryc[0, 0:24, :]
    for k in range(1, 8):
        total = total + ryc[k, 0:24, :]
    rz[z] = total
    for dz in range(1, NZ):
        three(dz).start()
    pump(4)
    for dz in range(1, NZ):
        three(dz).wait_recv()
    pump(5)
    total = rz[0]
    for k in range(1, NZ):
        total = total + rz[k]
    fin[x, pl.ds(pl.multiple_of(24 * (y * 2 + c), 8), 24), :] = total
    for k in range(1, 8):
        four(k).start()
    pump(6)
    for k in range(1, 8):
        four(k).wait_recv()
    for dx in range(1, NX):
        five(dx).start()
    pump(7)
    for dx in range(1, NX):
        five(dx).wait_recv()

    def exact(a, b, dims):
        return lax.dot_general(a, b, (dims, ((), ())), precision=HIGH, preferred_element_type=F32)

    factor = 1.0 / (128 * 64**0.5)
    sides = [(s, q) for s in range(3) for q in range(2)]

    def sums(s, q):
        if s < 2:
            return jnp.concatenate([fin[2 * q + k, 64 * s:64 * s + 64, :] for k in range(2)], axis=0)
        return jnp.concatenate([fin[k, 128 + 32 * q:160 + 32 * q, :] for k in range(NX)], axis=0)

    moved = [exact(pickers[s], sums(s, q), ((0,), (1,) if s == 2 else (0,))) for s, q in sides]
    for (s, q), part in zip(sides, moved):
        eout[s, q] = exact(part, pickers[s], ((1,), (0,))) * factor

    c_gone()
    x_gone()

    def g_gone(g, carry):
        for way in range(2):
            near(g, way).wait_send()
            far(g, way).wait_send()
        return carry

    lax.fori_loop(0, 8, g_gone, 0)
    for dx in range(1, NX):
        one(dx).wait_send()
        five(dx).wait_send()
    for k in range(1, 8):
        two(k).wait_send()
        three(k).wait_send()
        four(k).wait_send()

    def landed(part, k):
        return pltpu.make_async_remote_copy(
            src_ref=sg.at[pl.ds(0, per)], dst_ref=sgr.at[part, pl.ds(per * k, per)],
            send_sem=s_ss.at[0, k], recv_sem=s_rs.at[part, k],
            device_id=device(0, 0, 2, 0), device_id_type=MESH)

    for k in range(PIECES):
        for half in range(2):
            landed(half, k).wait_recv()
            back(half, k).wait_send()


def finish(back, sums, out, eout, outturn, sgr, given, held, in_s, out_s):
    per = 16 // STEPS
    come = pltpu.make_async_copy(sums, held, in_s.at[STEPS])
    go = pltpu.make_async_copy(held, eout, out_s.at[STEPS])

    def load(k):
        at = pl.ds(per * k, per)
        return pltpu.make_async_copy(back.at[:, at], sgr.at[:, at], in_s.at[k])

    def give(k):
        at = pl.ds(per * k, per)
        return pltpu.make_async_copy(given.at[at], out.at[at], out_s.at[k])

    for k in range(STEPS):
        load(k).start()
    come.start()
    outturn[...] = output_turn()
    for k in range(STEPS):
        load(k).wait()
        made = []
        for i in range(per):
            n, rows = per * k + 2 * (i // 2), slice(64 * (i % 2), 64 * (i % 2) + 64)
            sides = [jnp.concatenate([sgr[r, n + nn, rows, cc * 128:cc * 128 + 128] for r in range(2) for cc in range(2)], axis=0)
                     for nn in range(2)]
            made.append(dot(outturn[...], jnp.concatenate(sides, axis=1)).astype(BF))
        for i in range(per):
            n, at = per * k + 2 * (i // 2), slice(256 * (i % 2), 256 * (i % 2) + 256)
            given[n, at, :] = made[i][:, :128]
            given[n + 1, at, :] = made[i][:, 128:]
        give(k).start()
        if k == 0:
            come.wait()
            go.start()
    for k in range(STEPS):
        give(k).wait()
    go.wait()


def local(initial_state, cotangent, gate_bank, slice_index, mode_order):
    hbm = pl.BlockSpec(memory_space=pl.ANY)
    vm = pl.BlockSpec(memory_space=pltpu.VMEM)
    sm = pl.BlockSpec(memory_space=pltpu.SMEM)
    big = lambda *shape: pltpu.VMEM(shape, BF)
    wide = lambda *shape: pltpu.VMEM(shape, F32)
    sem = lambda *shape: pltpu.SemaphoreType.DMA(shape)
    backs, sums = pl.pallas_call(
        kernel,
        out_shape=(jax.ShapeDtypeStruct((2, 16, 128, 256), BF), jax.ShapeDtypeStruct((3, 2, 128, 128), F32)),
        in_specs=[hbm, hbm, hbm, sm, sm],
        out_specs=(hbm, vm),
        scratch_shapes=[
            big(16, 4, 128, 128), big(16, 4, 128, 128), big(3, 4, 2, 128, 128), wide(3, 128, 128),
            big(256, 256), big(256, 256), big(256, 256), big(256, 256), big(64, 256), big(256, 256), big(256, 256),
            big(4, 2, 8, 4, 16, 256), big(4, 2, 8, 4, 16, 256), big(8, 8, 4, 16, 256), big(8, 8, 4, 16, 256), big(8, 128, 16, 256), big(2, 128, 16, 256),
            big(128, 32, 256), big(32, 128, 256), big(32, 128, 256), big(32, 128, 256),
            big(32, 128, 256), big(32, 128, 256),
            wide(4, 128, 128), wide(4, 128, 128), wide(9, 192, 128), wide(8, 24, 128), wide(4, 192, 128),
            sem(3), sem(8), sem(8), sem(8), sem(8), sem(8, 8), sem(8, 8), sem(8, 8), sem(8, 8), sem(8), sem(8), sem(2, 8), sem(2, 8), sem(2, 8), sem(2, 8), sem(2, PIECES), sem(2, PIECES),
            sem(4), sem(4), sem(8), sem(8), sem(8), sem(8), sem(8), sem(8), sem(4), sem(4),
        ],
        compiler_params=pltpu.CompilerParams(collective_id=0, has_side_effects=True, vmem_limit_bytes=54 << 20),
        name="gradients",
    )(
        cotangent.reshape(16, 4, 128, 128), initial_state.reshape(16, 4, 128, 128),
        gate_bank, slice_index, mode_order,
    )
    out, grads = pl.pallas_call(
        finish,
        out_shape=(jax.ShapeDtypeStruct((16, 512, 128), BF), jax.ShapeDtypeStruct((3, 2, 128, 128), F32)),
        in_specs=[hbm, hbm],
        out_specs=(hbm, hbm),
        scratch_shapes=[big(256, 256), big(2, 16, 128, 256), big(16, 512, 128), wide(3, 2, 128, 128), sem(STEPS + 1), sem(STEPS + 1)],
        compiler_params=pltpu.CompilerParams(vmem_limit_bytes=60 << 20),
        name="outputs",
    )(backs, sums)
    return grads, out.reshape(16, 128, 2, 2, 128)


def solution(mesh):
    in_specs = (P("grp", "mem", None, None, None), P("grp", "mem", None, None, None), P(), P(), P())
    out_specs = (P(), P("grp", None, "mem", None, None))
    return jax.shard_map(local, mesh=mesh, in_specs=in_specs, out_specs=out_specs, check_vma=False)
```
